32 devices in a mesh: views: 8 (over y, x, core), rows: 4 (over z).
Axes of the slice: x: 2, y: 2, z: 4, core: 2. Of those that a mesh axis runs over, the one named last changes fastest.
Arguments:
- projections: float32 [128, 8, 4096], P('views', 'rows'), may hold values from 0.0002 to 1.2, as said below
- partner: int32 [64], replicated, may hold values from 64 to 127, as said below
- geometry: int32 [2, 8], replicated, may hold values from 0 to 512, as said below
Outputs:
- sinogram: float32 [64, 8, 7680], P('views', 'rows')
The draws below stay inside these ranges and needn't reach their ends.
Inputs may be any that keep to these rules, and one draw needn't show every extreme that they name: Each value appears once, and partner[j] - 64 lies in the same aligned block of 16 views as j. geometry[0, r] lies between 256 and 512; geometry[1, r] lies between 0 and 512 - geometry[0, r]. `projections`: positive transmissions.
All inputs are finite; a program needn't handle non-finite values.
Results may differ from the reference program's by a relative error of at most 0.0003.
Values sent between devices are 32-bit elements; how exact they have to be, the bound alone decides.
A program may use at most 64 MiB of HBM per device.

```python
import math
import jax
import jax.numpy as jnp
from jax import lax

COLS = 4096
OVMAX = 512
OVMIN = 256
VIEW_DEV = 16
GBAND = 4
VIEWS = 128
HALF = 64
ROWS = 8
WIDE = 7680
N_VIEWS = 8


def draw_projections(key, part):
    key_rough, key_stripe = jax.random.split(key, 2)
    shape = (VIEWS, ROWS, COLS)
    view_ids = jnp.arange(VIEWS)[:, None, None]
    row_frac = jnp.arange(ROWS)[None, :, None].astype(jnp.float32) / max(ROWS - 1, 1)
    col_frac = jnp.arange(COLS)[None, None, :].astype(jnp.float32) / COLS
    col_exp = jnp.where(view_ids < HALF, 0.5 + 0.5 * col_frac, 0.5 - 0.5 * col_frac)
    amplitude = 0.04 * 10.0 ** (col_exp + row_frac)
    rough = jax.random.uniform(key_rough, shape, jnp.float32, 0.5, 1.5)
    stripes = 0.02 * jax.random.truncated_normal(key_stripe, -5.0, 5.0, (1, ROWS, COLS), jnp.float32)
    thickness = amplitude * rough + stripes
    return jnp.exp(-thickness).astype(jnp.float32)


def draw_partner(key, part):
    blocks = HALF // VIEW_DEV
    keys = jax.random.split(key, blocks)
    orders = jax.vmap(lambda single: jax.random.permutation(single, VIEW_DEV))(keys)
    starts = jnp.arange(blocks)[:, None] * VIEW_DEV
    return (HALF + starts + orders).reshape(HALF).astype(jnp.int32)


def draw_geometry(key, part):
    key_width, key_offset, key_pick = jax.random.split(key, 3)
    margin = jax.random.randint(key_width, (ROWS,), OVMIN, OVMAX + 1)
    picks = jax.random.permutation(key_pick, ROWS)
    margin = margin.at[picks[0]].set(OVMAX).at[picks[1]].set(OVMIN)
    offset = jax.random.randint(key_offset, (ROWS,), 0, OVMAX - margin + 1)
    offset = offset.at[picks[1]].set(OVMAX - OVMIN).at[picks[0]].set(0)
    return jnp.stack([margin, offset]).astype(jnp.int32)


def setup_inputs(seed: int = 0) -> dict:
    arg_keys = jax.random.split(jax.random.key(seed), 4)
    return {
        "projections": draw_projections(jax.random.fold_in(arg_keys[3], 71), 0),
        "partner": draw_partner(jax.random.fold_in(arg_keys[3], 71), 0),
        "geometry": draw_geometry(jax.random.fold_in(arg_keys[3], 71), 0),
    }


phase_strength = 2.0
shrink_floor = 1e-6


def angle_grid(left_ids, right_ids, period):
    product = (left_ids[:, None] * right_ids[None, :]) % period
    return (2.0 * math.pi / period) * product.astype(jnp.float32)


def band_tables(view_ids, half_count, gband):
    freqs = jnp.arange(gband).astype(jnp.int32)
    angles = angle_grid(view_ids.astype(jnp.int32), freqs, half_count)
    forward = jnp.concatenate([jnp.cos(angles), -jnp.sin(angles[:, 1:])], axis=1)
    doubling = jnp.where(freqs == 0, 1.0, 2.0).astype(jnp.float32)
    inverse = jnp.concatenate([doubling[None, :] * jnp.cos(angles), -2.0 * jnp.sin(angles[:, 1:])], axis=1)
    return forward, inverse.T / half_count


def phase_response(count):
    freqs = jnp.arange(count)
    return 1.0 / (1.0 + phase_strength * (2.0 * jnp.sin(math.pi * freqs.astype(jnp.float32) / count)) ** 2)


def ramp_response(count):
    freqs = jnp.arange(count)
    return 2.0 * jnp.minimum(freqs, count - freqs).astype(jnp.float32) / count


def circular_apply(lines, response):
    spectrum = jnp.fft.fft(lines, axis=-1) * response
    return jnp.real(jnp.fft.ifft(spectrum, axis=-1)).astype(lines.dtype)


def stitch_row(first_row, second_row, margin, offset):
    positions = jnp.arange(WIDE) + offset
    weight = jnp.clip(((positions - COLS + margin).astype(jnp.float32) + 0.5) / margin.astype(jnp.float32), 0.0, 1.0)
    partner_cols = COLS - 1 - positions
    partner_part = jnp.where(partner_cols >= 0, jnp.take(second_row, jnp.clip(partner_cols, 0, COLS - 1), axis=1), 0.0)
    own_cols = positions - COLS + margin
    own_part = jnp.where(own_cols >= 0, jnp.take(first_row, jnp.clip(own_cols, 0, COLS - 1), axis=1), 0.0)
    return (1.0 - weight) * partner_part + weight * own_part


def reference(projections, partner, geometry):
    def prepare(pair):
        row_data, row_geo = pair
        attenuation = -jnp.log(circular_apply(row_data, phase_response(COLS)))
        first_rows = attenuation[:HALF]
        second_rows = jnp.take(attenuation, partner, axis=0)
        return stitch_row(first_rows, second_rows, row_geo[0], row_geo[1])

    stitched = lax.map(prepare, (jnp.moveaxis(projections, 1, 0), geometry.T))
    forward, inverse = band_tables(jnp.arange(HALF), HALF, GBAND)
    coeff = jnp.einsum("rjc,jk->krc", stitched, forward, precision=lax.Precision.HIGHEST)
    real_part = coeff[:GBAND]
    imag_part = jnp.concatenate([jnp.zeros_like(coeff[:1]), coeff[GBAND:]], axis=0)
    magnitude = real_part * real_part + imag_part * imag_part
    power = jnp.mean(magnitude, axis=(1, 2)) + shrink_floor
    weights = 1.0 - (jnp.arange(GBAND).astype(jnp.float32) / GBAND) ** 2
    factor = weights[:, None, None] * magnitude / (magnitude + power[:, None, None])
    kept = jnp.concatenate([factor * real_part, (factor * imag_part)[1:]], axis=0)
    cleaned = stitched - jnp.einsum("krc,kj->rjc", kept, inverse, precision=lax.Precision.HIGHEST)
    filtered = lax.map(lambda lines: circular_apply(lines, ramp_response(WIDE)), cleaned)
    ordered = jnp.moveaxis(filtered, 0, 1).reshape(N_VIEWS // 2, 2, VIEW_DEV // 2, ROWS, WIDE)
    return jnp.swapaxes(ordered, 0, 1).reshape(HALF, ROWS, WIDE)
```

```python
import functools
import math

import jax
import jax.numpy as jnp
import numpy as np
from jax import lax
from jax.experimental import pallas as pl
from jax.experimental.pallas import tpu as pltpu
from jax.sharding import PartitionSpec as P

GBAND = 4
WIDE = 7680
LANES = 128
TURNS = WIDE // LANES
PAD = 32
NCOEF = 2 * GBAND - 1
SLOT = 8

SHRINK_FLOOR = 1e-06
MESH = pl.DeviceIdType.MESH


def each(count, body):
    if count <= 16:
        for i in range(count):
            body(i)
    else:
        lax.fori_loop(0, count, lambda i, c: (body(i), c)[1], 0)


def split_np(table):
    hi = np.asarray(table, np.float32).astype(jnp.bfloat16)
    lo = (np.asarray(table, np.float64) - hi.astype(np.float64)).astype(jnp.bfloat16)
    return hi, lo


def split(x):
    hi = x.astype(jnp.bfloat16)
    lo = (x - hi.astype(jnp.float32)).astype(jnp.bfloat16)
    return hi, lo


def phase_table():
    i = np.arange(LANES)[:, None]
    j = np.arange(LANES)[None, :]
    parts = []
    for apart in (0, 1, -1):
        dist = np.abs(LANES * apart + j - i)
        parts.append(np.where(dist <= 126, np.exp2(-np.minimum(dist, 126).astype(np.float64)), 0.0))
    one = np.concatenate(parts, axis=1)
    return np.stack([one, one[::-1]]).astype(jnp.bfloat16)


def ramp_tables(left_blocks, right_start):
    k = np.arange(PAD)
    a = np.concatenate([np.arange(left_blocks), right_start + np.arange(left_blocks)])
    live = (k <= TURNS // 2)[:, None]
    ang = 2.0 * math.pi / TURNS * ((k[:, None] * a[None, :]) % TURNS)
    first = np.concatenate([np.where(live, np.cos(ang), 0), np.where(live, -np.sin(ang), 0)])
    fhi, flo = split_np(first)
    first = np.concatenate([fhi, fhi, flo], axis=1)
    b = np.arange(LANES)
    ang = 2.0 * math.pi / LANES * ((b[:, None] * b[None, :]) % LANES)
    c, s = np.cos(ang), np.sin(ang)
    fwd = split_np(np.block([[c, -s], [s, c]]))
    inv = split_np(np.block([[c, s], [-s, c]]))
    ang = 2.0 * math.pi / WIDE * ((k[:, None] * b[None, :]) % WIDE)
    twist = np.stack([np.cos(ang), np.sin(ang)]).astype(np.float32)
    freq = TURNS * b[None, :] + k[:, None]
    times = np.where((k == 0) | (k == TURNS // 2), 1.0, 2.0)[:, None]
    response = np.where(live, 2.0 * np.minimum(freq, WIDE - freq) / WIDE * times / WIDE, 0.0)
    a = np.arange(64)
    ang = 2.0 * math.pi / TURNS * ((a[:, None] * k[None, :]) % TURNS)
    last = np.concatenate([np.cos(ang), -np.sin(ang)], axis=1) * np.concatenate([live, live])[:, 0]
    lhi, llo = split_np(last)
    last = np.concatenate([lhi, lhi, llo], axis=1)
    return first, np.stack(fwd), np.stack(inv), twist, response.astype(np.float32), last


def band_tables(half_total):
    j = np.arange(half_total)[:, None]
    g = np.arange(GBAND)[None, :]
    ang = 2.0 * math.pi / half_total * ((j * g) % half_total)
    zero = np.zeros((half_total, 1))
    fwd = np.concatenate([np.cos(ang), -np.sin(ang[:, 1:]), zero], axis=1)
    dbl = np.where(g == 0, 1.0, 2.0)
    inv = np.concatenate([dbl * np.cos(ang), -2.0 * np.sin(ang[:, 1:]), zero], axis=1) / half_total
    return np.concatenate([fwd, inv], axis=1).reshape(-1).astype(np.float32)


def dot(a, b):
    return jnp.dot(a, b, preferred_element_type=jnp.float32)


def kernel(
    n, nr, views, blocks, rows_total,
    partner, geometry, band, x_ref, phase_ref, first_ref, fwd_ref, inv_ref, twist_ref, resp_ref, last_ref,
    out_ref,
    st, cbuf, rsbuf, agbuf, full, pwbuf, mid, mv, z,
    ex_send, ex_recv, rs_send, rs_recv, ag_send, ag_recv, pw_send, pw_recv,
):
    half = n // 2
    paired = views // 2
    me = lax.axis_index("views")
    my_row = lax.axis_index("rows")
    upper = me >= half
    up = jnp.where(upper, 1, 0)
    s = lax.rem(me, half)
    side = 1 - up
    other = lax.rem(me + half, n)
    strip = cbuf.shape[0] // half
    cols = blocks * LANES
    vrows = 2 * blocks

    barrier = pltpu.get_barrier_semaphore()

    def greet_view(d):
        pl.semaphore_signal(barrier, inc=1, device_id={"views": lax.rem(me + d + 1, n)}, device_id_type=MESH)

    def greet_row(d):
        pl.semaphore_signal(barrier, inc=1, device_id={"rows": lax.rem(my_row + d + 1, nr)}, device_id_type=MESH)

    each(n - 1, greet_view)
    each(nr - 1, greet_row)

    margins = [geometry[0, my_row * 2 + r] for r in range(2)]
    offsets = [geometry[1, my_row * 2 + r] for r in range(2)]
    move = [jnp.where(upper, cols - offsets[r], 2 * cols - WIDE - margins[r] - offsets[r]) for r in range(2)]
    whole = [move[r] // LANES for r in range(2)]
    rest = [move[r] - whole[r] * LANES for r in range(2)]
    ri = lax.broadcasted_iota(jnp.int32, (vrows, vrows), 0)
    ci = lax.broadcasted_iota(jnp.int32, (vrows, vrows), 1)
    second = ri >= blocks
    a_id = jnp.where(second, ri - blocks, ri)
    a_id = a_id - jnp.where(second, whole[1], whole[0])
    a_id = jnp.where(a_id < 0, a_id + blocks, a_id)
    a_id = jnp.where(upper, blocks - 1 - a_id, a_id)
    pick = (ci == 2 * a_id + jnp.where(second, 1, 0)).astype(jnp.float32).astype(jnp.bfloat16)

    rl = lax.broadcasted_iota(jnp.int32, (vrows, LANES), 0)
    lane = lax.broadcasted_iota(jnp.int32, (vrows, LANES), 1)
    sec = rl >= blocks
    t = jnp.where(sec, rl - blocks, rl) * LANES + lane + jnp.where(upper, 0, WIDE - cols)
    offs = jnp.where(sec, offsets[1], offsets[0])
    marg = jnp.where(sec, margins[1], margins[0])
    ramp = ((t + offs - cols + marg).astype(jnp.float32) + 0.5) / marg.astype(jnp.float32)
    w = jnp.minimum(jnp.maximum(ramp, 0.0), 1.0)
    weight = jnp.where(upper, 1.0 - w, w)
    lane_b = lax.broadcasted_iota(jnp.int32, (blocks, LANES), 1)

    half_total = views * half
    base = s * views
    r128 = lax.broadcasted_iota(jnp.int32, (LANES, LANES), 0)
    c128 = lax.broadcasted_iota(jnp.int32, (LANES, LANES), 1)
    one = phase_ref[up]
    phases = []
    for r in range(2):
        to = r128 + rest[r]
        to = jnp.where(to >= LANES, to - LANES, to)
        turn = (to == c128).astype(jnp.float32).astype(jnp.bfloat16)
        turned = [dot(one[:, p * LANES:(p + 1) * LANES], turn) for p in range(3)]
        turned = jnp.concatenate(turned, axis=1).astype(jnp.bfloat16)
        phases.append(jnp.concatenate([turned] * 3, axis=0))

    def place(start, sent):
        for v in range(paired):
            i = start + v
            src = jnp.where(upper, partner[base + i] - half_total - base, i)
            x = x_ref[jnp.minimum(jnp.maximum(src, 0), views - 1)]
            hi = x.astype(jnp.bfloat16)
            left = x - hi.astype(jnp.float32)
            md = left.astype(jnp.bfloat16)
            lo = (left - md.astype(jnp.float32)).astype(jnp.bfloat16)
            moved = dot(pick, jnp.concatenate([hi, md, lo], axis=1)).astype(jnp.bfloat16)
            for r in range(2):
                mv[r, v * blocks:(v + 1) * blocks, :] = moved[r * blocks:(r + 1) * blocks]
        for r in range(2):
            z[r] = dot(mv[r], phases[r])
        for v in range(paired):
            lines = []
            for r in range(2):
                rows = slice(v * blocks, (v + 1) * blocks)
                y = (
                    z[r, rows, :LANES]
                    + pltpu.roll(z[r, rows, LANES:2 * LANES], 1, 0)
                    + pltpu.roll(z[r, rows, 2 * LANES:], blocks - 1, 0)
                )
                y = -jnp.log(y * (1.0 / 3.0))
                y = jnp.where(lane_b < rest[r], pltpu.roll(y, 1, 0), y)
                lines.append(y)
            st[side, start + v] = weight * jnp.concatenate(lines, axis=0)
            if sent:
                ex_copy(v).start()

    def ex_copy(v):
        i = (1 - up) * paired + v
        return pltpu.make_async_remote_copy(
            src_ref=st.at[side, i], dst_ref=st.at[side, i],
            send_sem=ex_send.at[v], recv_sem=ex_recv.at[v],
            device_id={"views": other}, device_id_type=MESH)

    pl.semaphore_wait(barrier, n + nr - 2)
    place((1 - up) * paired, True)
    place(up * paired, False)

    for k in range(NCOEF):
        acc = None
        for i in range(views):
            term = band[(base + i) * 16 + k] * st[side, i]
            acc = term if acc is None else acc + term
        cbuf[pl.ds(k, vrows, stride=SLOT), :] = acc
    cbuf[pl.ds(NCOEF, vrows, stride=SLOT), :] = jnp.zeros((vrows, LANES), jnp.float32)

    def rs_copy(d):
        to = lax.rem(s + d + 1, half)
        return pltpu.make_async_remote_copy(
            src_ref=cbuf.at[pl.ds(pl.multiple_of(to * strip, 8), strip)], dst_ref=rsbuf.at[d],
            send_sem=rs_send.at[d], recv_sem=rs_recv.at[d],
            device_id={"views": up * half + to}, device_id_type=MESH)

    each(half - 1, lambda d: rs_copy(d).start())
    agbuf[me] = cbuf[pl.ds(pl.multiple_of(s * strip, 8), strip), :]

    def rs_add(d):
        rs_copy(d).wait_recv()
        agbuf[me] = agbuf[me] + rsbuf[d]

    each(half - 1, rs_add)

    def ag_copy(d):
        return pltpu.make_async_remote_copy(
            src_ref=agbuf.at[me], dst_ref=agbuf.at[me],
            send_sem=ag_send.at[d], recv_sem=ag_recv.at[d],
            device_id={"views": lax.rem(me + d + 1, n)}, device_id_type=MESH)

    each(n - 1, lambda d: ag_copy(d).start())
    each(half - 1, lambda d: rs_copy(d).wait_send())

    def ag_arrive(d):
        frm = lax.rem(me + n - d - 1, n)
        pltpu.make_async_remote_copy(
            src_ref=agbuf.at[frm], dst_ref=agbuf.at[frm],
            send_sem=ag_send.at[d], recv_sem=ag_recv.at[d],
            device_id={"views": frm}, device_id_type=MESH).wait_recv()

    each(n - 1, ag_arrive)
    each(n - 1, lambda d: ag_copy(d).wait_send())

    lap = 2 * blocks - TURNS
    strips_side = agbuf.shape[0] // 2
    flat = agbuf
    rows_id = lax.broadcasted_iota(jnp.int32, (2 * blocks, LANES), 0)
    joins = jnp.logical_and(rows_id >= blocks - lap, rows_id < blocks)
    gone = jnp.logical_and(rows_id >= blocks, rows_id < blocks + lap)
    sums = [jnp.zeros((1, LANES), jnp.float32) for _ in range(GBAND)]
    for k in range(NCOEF):
        pieces = {}
        for sd in range(2):
            first_slot = half if sd == 0 else 0
            per = strip // SLOT
            if per >= 8:
                got = [flat[first_slot + q, pl.ds(k, per, stride=SLOT), :] for q in range(half)]
                pieces[sd] = jnp.concatenate(got, axis=0)
            else:
                got = [flat[first_slot + q, pl.ds(k, per), :] for q in range(half)]
                pieces[sd] = jnp.concatenate(got, axis=0)
        for r in range(2):
            line = jnp.concatenate([pieces[0][r * blocks:(r + 1) * blocks],
                                    pieces[1][r * blocks:(r + 1) * blocks]], axis=0)
            ahead = pltpu.roll(line, 2 * blocks - lap, 0)
            line = jnp.where(joins, line + ahead, jnp.where(gone, 0.0, line))
            full[k, r] = line
            g = k if k < GBAND else k - GBAND + 1
            sums[g] = sums[g] + jnp.sum(line * line, axis=0, keepdims=True)
    pwbuf[0] = jnp.concatenate(sums + [jnp.zeros((8 - GBAND, LANES), jnp.float32)], axis=0)

    def pw_copy(d):
        return pltpu.make_async_remote_copy(
            src_ref=pwbuf.at[0], dst_ref=pwbuf.at[d + 1],
            send_sem=pw_send.at[d], recv_sem=pw_recv.at[d],
            device_id={"rows": lax.rem(my_row + d + 1, nr)}, device_id_type=MESH)

    each(nr - 1, lambda d: pw_copy(d).start())
    for v in range(paired):
        ex_copy(v).wait_send()
    for v in range(paired):
        i = up * paired + v
        pltpu.make_async_remote_copy(
            src_ref=st.at[1 - side, i], dst_ref=st.at[1 - side, i],
            send_sem=ex_send.at[v], recv_sem=ex_recv.at[v],
            device_id={"views": other}, device_id_type=MESH).wait_recv()
    each(nr - 1, lambda d: pw_copy(d).wait_recv())
    total = pwbuf[0]
    for d in range(nr - 1):
        total = total + pwbuf[d + 1]
    power = jnp.sum(total, axis=1, keepdims=True) / (rows_total * WIDE) + SHRINK_FLOOR
    for r in range(2):
        for g in range(GBAND):
            re = full[g, r]
            mag = re * re
            if g:
                im = full[GBAND + g - 1, r]
                mag = mag + im * im
            factor = (1.0 - (g / GBAND) ** 2) * mag / (mag + power[g:g + 1])
            full[g, r] = factor * re
            if g:
                full[GBAND + g - 1, r] = factor * im
    each(nr - 1, lambda d: pw_copy(d).wait_send())

    cos, sin = twist_ref[0], twist_ref[1]
    first = first_ref[...]
    for v in range(paired):
        i = up * paired + v
        lines = []
        for r in range(2):
            line = jnp.concatenate([st[0, i, r * blocks:(r + 1) * blocks],
                                    st[1, i, r * blocks:(r + 1) * blocks]], axis=0)
            for k in range(NCOEF):
                line = line - band[(base + i) * 16 + 8 + k] * full[k, r]
            lines.append(line)
        hi, lo = split(jnp.concatenate(lines, axis=1))
        step = dot(first, jnp.concatenate([hi, lo, hi], axis=0))
        for r in range(2):
            re = step[:PAD, r * LANES:(r + 1) * LANES]
            im = step[PAD:, r * LANES:(r + 1) * LANES]
            at = (2 * v + r) * PAD
            mid[at:at + PAD, :LANES] = re * cos + im * sin
            mid[at:at + PAD, LANES:] = im * cos - re * sin

    hi, lo = split(mid[...])
    spec = dot(hi, fwd_ref[0]) + dot(lo, fwd_ref[0]) + dot(hi, fwd_ref[1])
    resp = resp_ref[...]
    resp = jnp.concatenate([resp, resp], axis=1)
    resp = jnp.concatenate([resp] * (2 * paired), axis=0)
    hi, lo = split(spec * resp)
    mid[...] = dot(hi, inv_ref[0]) + dot(lo, inv_ref[0]) + dot(hi, inv_ref[1])

    last = last_ref[...]
    for v in range(paired):
        res, ims = [], []
        for r in range(2):
            at = (2 * v + r) * PAD
            re = mid[at:at + PAD, :LANES]
            im = mid[at:at + PAD, LANES:]
            res.append(re * cos - im * sin)
            ims.append(im * cos + re * sin)
        both = jnp.concatenate([jnp.concatenate(res, axis=1), jnp.concatenate(ims, axis=1)], axis=0)
        hi, lo = split(both)
        y = dot(last, jnp.concatenate([hi, lo, hi], axis=0))
        for r in range(2):
            out_ref[pl.ds(v * 2 * TURNS + r, TURNS, stride=2), :] = y[:TURNS, r * LANES:(r + 1) * LANES]


def on_device(n, nr, projections, partner, geometry):
    views, row_dev, cols = projections.shape
    assert row_dev == 2
    blocks = cols // LANES
    half = n // 2
    vrows = 2 * blocks
    strip = vrows * SLOT // half
    x = projections.reshape(views, row_dev, blocks, LANES).transpose(0, 2, 1, 3).reshape(views, vrows, LANES)
    tables = (phase_table(),) + ramp_tables(blocks, TURNS - blocks)
    band = jnp.asarray(band_tables(views * half))
    smem = pl.BlockSpec(memory_space=pltpu.SMEM)
    vmem = pl.BlockSpec(memory_space=pltpu.VMEM)
    paired = views // 2
    dma = pltpu.SemaphoreType.DMA
    out = pl.pallas_call(
        functools.partial(kernel, n, nr, views, blocks, row_dev * nr),
        out_shape=jax.ShapeDtypeStruct((paired * 2 * TURNS, LANES), jnp.float32),
        in_specs=[smem] * 3 + [vmem] * (1 + len(tables)),
        out_specs=vmem,
        scratch_shapes=[
            pltpu.VMEM((2, views, vrows, LANES), jnp.float32),
            pltpu.VMEM((vrows * SLOT, LANES), jnp.float32),
            pltpu.VMEM((half - 1, strip, LANES), jnp.float32),
            pltpu.VMEM((n, strip, LANES), jnp.float32),
            pltpu.VMEM((NCOEF, 2, 2 * blocks, LANES), jnp.float32),
            pltpu.VMEM((nr, 8, LANES), jnp.float32),
            pltpu.VMEM((paired * 2 * PAD, 2 * LANES), jnp.float32),
            pltpu.VMEM((2, paired * blocks, 3 * LANES), jnp.bfloat16),
            pltpu.VMEM((2, paired * blocks, 3 * LANES), jnp.float32),
            dma((paired,)), dma((paired,)),
            dma((half - 1,)), dma((half - 1,)),
            dma((n - 1,)), dma((n - 1,)),
            dma((nr - 1,)), dma((nr - 1,)),
        ],
        compiler_params=pltpu.CompilerParams(
            collective_id=0, has_side_effects=True, vmem_limit_bytes=32 * 2**20),
        cost_estimate=pl.CostEstimate(flops=10**9, bytes_accessed=2 * 10**6, transcendentals=131072),
    )(partner, geometry, band, x, *[jnp.asarray(t) for t in tables])
    out = out.reshape(paired, TURNS, 2, LANES).transpose(0, 2, 1, 3)
    return out.reshape(paired, 2, WIDE)


def solution(mesh):
    in_specs = (P("views", "rows", None), P(), P())
    out_specs = P("views", "rows", None)
    n, nr = mesh.shape["views"], mesh.shape["rows"]
    return jax.shard_map(
        functools.partial(on_device, n, nr), mesh=mesh, in_specs=in_specs, out_specs=out_specs, check_vma=False
    )
```

```python
import functools
import math

import jax
import jax.numpy as jnp
import numpy as np
from jax import lax
from jax.experimental import pallas as pl
from jax.experimental.pallas import tpu as pltpu
from jax.sharding import PartitionSpec as P

GBAND = 4
WIDE = 7680
LANES = 128
TURNS = WIDE // LANES
PAD = 32
NCOEF = 2 * GBAND - 1
SLOT = 8

SHRINK_FLOOR = 1e-06
MESH = pl.DeviceIdType.MESH


def each(count, body):
    if count <= 16:
        for i in range(count):
            body(i)
    else:
        lax.fori_loop(0, count, lambda i, c: (body(i), c)[1], 0)


def split_np(table):
    hi = np.asarray(table, np.float32).astype(jnp.bfloat16)
    lo = (np.asarray(table, np.float64) - hi.astype(np.float64)).astype(jnp.bfloat16)
    return hi, lo


def split(x):
    hi = x.astype(jnp.bfloat16)
    lo = (x - hi.astype(jnp.float32)).astype(jnp.bfloat16)
    return hi, lo


def phase_table():
    i = np.arange(LANES)[:, None]
    j = np.arange(LANES)[None, :]
    parts = []
    for apart in (0, 1, -1):
        dist = np.abs(LANES * apart + j - i)
        parts.append(np.where(dist <= 126, np.exp2(-np.minimum(dist, 126).astype(np.float64)), 0.0))
    one = np.concatenate(parts, axis=1)
    return np.stack([one, one[::-1]]).astype(jnp.bfloat16)


def ramp_tables(left_blocks, right_start):
    k = np.arange(PAD)
    a = np.concatenate([np.arange(left_blocks), right_start + np.arange(left_blocks)])
    live = (k <= TURNS // 2)[:, None]
    ang = 2.0 * math.pi / TURNS * ((k[:, None] * a[None, :]) % TURNS)
    first = np.concatenate([np.where(live, np.cos(ang), 0), np.where(live, -np.sin(ang), 0)])
    fhi, flo = split_np(first)
    first = np.concatenate([fhi, fhi, flo], axis=1)
    b = np.arange(LANES)
    ang = 2.0 * math.pi / LANES * ((b[:, None] * b[None, :]) % LANES)
    c, s = np.cos(ang), np.sin(ang)
    fwd = split_np(np.block([[c, -s], [s, c]]))
    inv = split_np(np.block([[c, s], [-s, c]]))
    ang = 2.0 * math.pi / WIDE * ((k[:, None] * b[None, :]) % WIDE)
    twist = np.stack([np.cos(ang), np.sin(ang)]).astype(np.float32)
    freq = TURNS * b[None, :] + k[:, None]
    times = np.where((k == 0) | (k == TURNS // 2), 1.0, 2.0)[:, None]
    response = np.where(live, 2.0 * np.minimum(freq, WIDE - freq) / WIDE * times / WIDE, 0.0)
    a = np.arange(64)
    ang = 2.0 * math.pi / TURNS * ((a[:, None] * k[None, :]) % TURNS)
    last = np.concatenate([np.cos(ang), -np.sin(ang)], axis=1) * np.concatenate([live, live])[:, 0]
    lhi, llo = split_np(last)
    last = np.concatenate([lhi, lhi, llo], axis=1)
    return first, twist, np.stack(fwd), response.astype(np.float32), np.stack(inv), last


def band_tables(half_total):
    j = np.arange(half_total)[:, None]
    g = np.arange(GBAND)[None, :]
    ang = 2.0 * math.pi / half_total * ((j * g) % half_total)
    zero = np.zeros((half_total, 1))
    fwd = np.concatenate([np.cos(ang), -np.sin(ang[:, 1:]), zero], axis=1)
    dbl = np.where(g == 0, 1.0, 2.0)
    inv = np.concatenate([dbl * np.cos(ang), -2.0 * np.sin(ang[:, 1:]), zero], axis=1) / half_total
    return np.concatenate([fwd, inv], axis=1).reshape(-1).astype(np.float32)


def dot(a, b):
    return jnp.dot(a, b, preferred_element_type=jnp.float32)


def kernel(
    n, nr, views, blocks, rows_total,
    partner_hbm, geometry_hbm, band_hbm, x_hbm, phase_hbm, first_hbm, twist_hbm, fwd_hbm, resp_hbm, inv_hbm, last_hbm,
    out_ref,
    partner, geometry, band, x_ref, phase_ref, first_ref, twist_ref, fwd_ref, resp_ref, inv_ref, last_ref, ld_sem,
    st, cbuf, rsbuf, agbuf, full, pwbuf, mid, mv, z,
    ex_send, ex_recv, rs_send, rs_recv, ag_send, ag_recv, fw_send, fw_recv, pw_send, pw_recv,
):
    half = n // 2
    paired = views // 2
    me = lax.axis_index("views")
    my_row = lax.axis_index("rows")
    upper = me >= half
    up = jnp.where(upper, 1, 0)
    s = lax.rem(me, half)
    side = 1 - up
    other = lax.rem(me + half, n)
    strip = cbuf.shape[0] // half
    cols = blocks * LANES
    vrows = 2 * blocks

    barrier = pltpu.get_barrier_semaphore()

    def greet_view(d):
        pl.semaphore_signal(barrier, inc=1, device_id={"views": lax.rem(me + d + 1, n)}, device_id_type=MESH)

    def greet_row(d):
        pl.semaphore_signal(barrier, inc=1, device_id={"rows": lax.rem(my_row + d + 1, nr)}, device_id_type=MESH)

    each(n - 1, greet_view)
    each(nr - 1, greet_row)

    sources = (geometry_hbm, partner_hbm, x_hbm, phase_hbm, band_hbm, first_hbm, twist_hbm, fwd_hbm, resp_hbm, inv_hbm,
               last_hbm)
    targets = (geometry, partner, x_ref, phase_ref, band, first_ref, twist_ref, fwd_ref, resp_ref, inv_ref, last_ref)
    loads = [pltpu.make_async_copy(a, b, ld_sem.at[i]) for i, (a, b) in enumerate(zip(sources, targets))]
    for load in loads:
        load.start()
    for load in loads[:4]:
        load.wait()

    margins = [geometry[0, my_row * 2 + r] for r in range(2)]
    offsets = [geometry[1, my_row * 2 + r] for r in range(2)]
    move = [jnp.where(upper, cols - offsets[r], 2 * cols - WIDE - margins[r] - offsets[r]) for r in range(2)]
    whole = [move[r] // LANES for r in range(2)]
    rest = [move[r] - whole[r] * LANES for r in range(2)]
    ri = lax.broadcasted_iota(jnp.int32, (vrows, vrows), 0)
    ci = lax.broadcasted_iota(jnp.int32, (vrows, vrows), 1)
    second = ri >= blocks
    a_id = jnp.where(second, ri - blocks, ri)
    a_id = a_id - jnp.where(second, whole[1], whole[0])
    a_id = jnp.where(a_id < 0, a_id + blocks, a_id)
    a_id = jnp.where(upper, blocks - 1 - a_id, a_id)
    pick = (ci == 2 * a_id + jnp.where(second, 1, 0)).astype(jnp.float32).astype(jnp.bfloat16)

    rl = lax.broadcasted_iota(jnp.int32, (vrows, LANES), 0)
    lane = lax.broadcasted_iota(jnp.int32, (vrows, LANES), 1)
    sec = rl >= blocks
    t = jnp.where(sec, rl - blocks, rl) * LANES + lane + jnp.where(upper, 0, WIDE - cols)
    offs = jnp.where(sec, offsets[1], offsets[0])
    marg = jnp.where(sec, margins[1], margins[0])
    ramp = ((t + offs - cols + marg).astype(jnp.float32) + 0.5) / marg.astype(jnp.float32)
    w = jnp.minimum(jnp.maximum(ramp, 0.0), 1.0)
    weight = jnp.where(upper, 1.0 - w, w)
    lane_b = lax.broadcasted_iota(jnp.int32, (blocks, LANES), 1)

    half_total = views * half
    base = s * views
    r128 = lax.broadcasted_iota(jnp.int32, (LANES, LANES), 0)
    c128 = lax.broadcasted_iota(jnp.int32, (LANES, LANES), 1)
    one = phase_ref[up]
    phases = []
    for r in range(2):
        to = r128 + rest[r]
        to = jnp.where(to >= LANES, to - LANES, to)
        turn = (to == c128).astype(jnp.float32).astype(jnp.bfloat16)
        turned = [dot(one[:, p * LANES:(p + 1) * LANES], turn) for p in range(3)]
        turned = jnp.concatenate(turned, axis=1).astype(jnp.bfloat16)
        phases.append(jnp.concatenate([turned] * 3, axis=0))

    def place(start, sent):
        for v in range(paired):
            i = start + v
            src = jnp.where(upper, partner[base + i] - half_total - base, i)
            x = x_ref[jnp.minimum(jnp.maximum(src, 0), views - 1)]
            hi = x.astype(jnp.bfloat16)
            left = x - hi.astype(jnp.float32)
            md = left.astype(jnp.bfloat16)
            lo = (left - md.astype(jnp.float32)).astype(jnp.bfloat16)
            moved = dot(pick, jnp.concatenate([hi, md, lo], axis=1)).astype(jnp.bfloat16)
            for r in range(2):
                mv[r, v * blocks:(v + 1) * blocks, :] = moved[r * blocks:(r + 1) * blocks]
        for r in range(2):
            z[r] = dot(mv[r], phases[r])
        for v in range(paired):
            lines = []
            for r in range(2):
                rows = slice(v * blocks, (v + 1) * blocks)
                y = (
                    z[r, rows, :LANES]
                    + pltpu.roll(z[r, rows, LANES:2 * LANES], 1, 0)
                    + pltpu.roll(z[r, rows, 2 * LANES:], blocks - 1, 0)
                )
                y = -jnp.log(y * (1.0 / 3.0))
                y = jnp.where(lane_b < rest[r], pltpu.roll(y, 1, 0), y)
                lines.append(y)
            st[side, start + v] = weight * jnp.concatenate(lines, axis=0)
            if sent:
                ex_copy(v).start()

    def ex_copy(v):
        i = (1 - up) * paired + v
        return pltpu.make_async_remote_copy(
            src_ref=st.at[side, i], dst_ref=st.at[side, i],
            send_sem=ex_send.at[v], recv_sem=ex_recv.at[v],
            device_id={"views": other}, device_id_type=MESH)

    pl.semaphore_wait(barrier, n + nr - 2)
    place((1 - up) * paired, True)
    place(up * paired, False)

    for load in loads[4:]:
        load.wait()
    for k in range(NCOEF):
        acc = None
        for i in range(views):
            term = band[(base + i) * 16 + k] * st[side, i]
            acc = term if acc is None else acc + term
        cbuf[pl.ds(k, vrows, stride=SLOT), :] = acc
    cbuf[pl.ds(NCOEF, vrows, stride=SLOT), :] = jnp.zeros((vrows, LANES), jnp.float32)

    def rs_copy(d):
        to = lax.rem(s + d + 1, half)
        return pltpu.make_async_remote_copy(
            src_ref=cbuf.at[pl.ds(pl.multiple_of(to * strip, 8), strip)], dst_ref=rsbuf.at[d],
            send_sem=rs_send.at[d], recv_sem=rs_recv.at[d],
            device_id={"views": up * half + to}, device_id_type=MESH)

    each(half - 1, lambda d: rs_copy(d).start())
    agbuf[me] = cbuf[pl.ds(pl.multiple_of(s * strip, 8), strip), :]

    def rs_add(d):
        rs_copy(d).wait_recv()
        agbuf[me] = agbuf[me] + rsbuf[d]

    each(half - 1, rs_add)

    par = lax.rem(me, 2)
    sibling = me + 1 - 2 * par

    def ag_copy(d, slot):
        return pltpu.make_async_remote_copy(
            src_ref=agbuf.at[slot], dst_ref=agbuf.at[slot],
            send_sem=ag_send.at[d], recv_sem=ag_recv.at[d],
            device_id={"views": lax.rem(me + 2 * d + 2, n)}, device_id_type=MESH)

    def fw_copy(d, slot):
        return pltpu.make_async_remote_copy(
            src_ref=agbuf.at[slot], dst_ref=agbuf.at[slot],
            send_sem=fw_send.at[d], recv_sem=fw_recv.at[d],
            device_id={"views": sibling}, device_id_type=MESH)

    def came(d):
        return lax.rem(me + n - 2 * d - 2, n)

    def came_sibling(d):
        return lax.rem(sibling + n - 2 * d - 2, n)

    each(half - 1, lambda d: ag_copy(d, me).start())
    fw_copy(half - 1, me).start()
    each(half - 1, lambda d: rs_copy(d).wait_send())

    def forward(d):
        ag_copy(d, came(d)).wait_recv()
        fw_copy(d, came(d)).start()

    each(half - 1, forward)
    fw_copy(half - 1, sibling).wait_recv()
    each(half - 1, lambda d: fw_copy(d, came_sibling(d)).wait_recv())
    each(half - 1, lambda d: ag_copy(d, me).wait_send())
    each(half - 1, lambda d: fw_copy(d, came(d)).wait_send())
    fw_copy(half - 1, me).wait_send()

    lap = 2 * blocks - TURNS
    strips_side = agbuf.shape[0] // 2
    flat = agbuf
    rows_id = lax.broadcasted_iota(jnp.int32, (2 * blocks, LANES), 0)
    joins = jnp.logical_and(rows_id >= blocks - lap, rows_id < blocks)
    gone = jnp.logical_and(rows_id >= blocks, rows_id < blocks + lap)
    sums = [jnp.zeros((1, LANES), jnp.float32) for _ in range(GBAND)]
    for k in range(NCOEF):
        pieces = {}
        for sd in range(2):
            first_slot = half if sd == 0 else 0
            per = strip // SLOT
            if per >= 8:
                got = [flat[first_slot + q, pl.ds(k, per, stride=SLOT), :] for q in range(half)]
                pieces[sd] = jnp.concatenate(got, axis=0)
            else:
                got = [flat[first_slot + q, pl.ds(k, per), :] for q in range(half)]
                pieces[sd] = jnp.concatenate(got, axis=0)
        for r in range(2):
            line = jnp.concatenate([pieces[0][r * blocks:(r + 1) * blocks],
                                    pieces[1][r * blocks:(r + 1) * blocks]], axis=0)
            ahead = pltpu.roll(line, 2 * blocks - lap, 0)
            line = jnp.where(joins, line + ahead, jnp.where(gone, 0.0, line))
            full[k, r] = line
            g = k if k < GBAND else k - GBAND + 1
            sums[g] = sums[g] + jnp.sum(line * line, axis=0, keepdims=True)
    pwbuf[0] = jnp.concatenate(sums + [jnp.zeros((8 - GBAND, LANES), jnp.float32)], axis=0)

    def pw_copy(d):
        return pltpu.make_async_remote_copy(
            src_ref=pwbuf.at[0], dst_ref=pwbuf.at[d + 1],
            send_sem=pw_send.at[d], recv_sem=pw_recv.at[d],
            device_id={"rows": lax.rem(my_row + d + 1, nr)}, device_id_type=MESH)

    each(nr - 1, lambda d: pw_copy(d).start())
    for v in range(paired):
        ex_copy(v).wait_send()
    for v in range(paired):
        i = up * paired + v
        pltpu.make_async_remote_copy(
            src_ref=st.at[1 - side, i], dst_ref=st.at[1 - side, i],
            send_sem=ex_send.at[v], recv_sem=ex_recv.at[v],
            device_id={"views": other}, device_id_type=MESH).wait_recv()
    each(nr - 1, lambda d: pw_copy(d).wait_recv())
    total = pwbuf[0]
    for d in range(nr - 1):
        total = total + pwbuf[d + 1]
    power = jnp.sum(total, axis=1, keepdims=True) / (rows_total * WIDE) + SHRINK_FLOOR
    for r in range(2):
        for g in range(GBAND):
            re = full[g, r]
            mag = re * re
            if g:
                im = full[GBAND + g - 1, r]
                mag = mag + im * im
            factor = (1.0 - (g / GBAND) ** 2) * mag / (mag + power[g:g + 1])
            full[g, r] = factor * re
            if g:
                full[GBAND + g - 1, r] = factor * im
    each(nr - 1, lambda d: pw_copy(d).wait_send())

    cos, sin = twist_ref[0], twist_ref[1]
    first = first_ref[...]
    for v in range(paired):
        i = up * paired + v
        lines = []
        for r in range(2):
            line = jnp.concatenate([st[0, i, r * blocks:(r + 1) * blocks],
                                    st[1, i, r * blocks:(r + 1) * blocks]], axis=0)
            for k in range(NCOEF):
                line = line - band[(base + i) * 16 + 8 + k] * full[k, r]
            lines.append(line)
        hi, lo = split(jnp.concatenate(lines, axis=1))
        step = dot(first, jnp.concatenate([hi, lo, hi], axis=0))
        for r in range(2):
            re = step[:PAD, r * LANES:(r + 1) * LANES]
            im = step[PAD:, r * LANES:(r + 1) * LANES]
            at = (2 * v + r) * PAD
            mid[at:at + PAD, :LANES] = re * cos + im * sin
            mid[at:at + PAD, LANES:] = im * cos - re * sin

    hi, lo = split(mid[...])
    spec = dot(hi, fwd_ref[0]) + dot(lo, fwd_ref[0]) + dot(hi, fwd_ref[1])
    resp = resp_ref[...]
    resp = jnp.concatenate([resp, resp], axis=1)
    resp = jnp.concatenate([resp] * (2 * paired), axis=0)
    hi, lo = split(spec * resp)
    mid[...] = dot(hi, inv_ref[0]) + dot(lo, inv_ref[0]) + dot(hi, inv_ref[1])

    last = last_ref[...]
    for v in range(paired):
        res, ims = [], []
        for r in range(2):
            at = (2 * v + r) * PAD
            re = mid[at:at + PAD, :LANES]
            im = mid[at:at + PAD, LANES:]
            res.append(re * cos - im * sin)
            ims.append(im * cos + re * sin)
        both = jnp.concatenate([jnp.concatenate(res, axis=1), jnp.concatenate(ims, axis=1)], axis=0)
        hi, lo = split(both)
        y = dot(last, jnp.concatenate([hi, lo, hi], axis=0))
        for r in range(2):
            out_ref[pl.ds(v * 2 * TURNS + r, TURNS, stride=2), :] = y[:TURNS, r * LANES:(r + 1) * LANES]


def on_device(n, nr, projections, partner, geometry):
    views, row_dev, cols = projections.shape
    assert row_dev == 2
    blocks = cols // LANES
    half = n // 2
    vrows = 2 * blocks
    strip = vrows * SLOT // half
    x = projections.reshape(views, row_dev, blocks, LANES).transpose(0, 2, 1, 3).reshape(views, vrows, LANES)
    tables = (phase_table(),) + ramp_tables(blocks, TURNS - blocks)
    band = jnp.asarray(band_tables(views * half))
    vmem = pl.BlockSpec(memory_space=pltpu.VMEM)
    paired = views // 2
    dma = pltpu.SemaphoreType.DMA
    out = pl.pallas_call(
        functools.partial(kernel, n, nr, views, blocks, row_dev * nr),
        out_shape=jax.ShapeDtypeStruct((paired * 2 * TURNS, LANES), jnp.float32),
        in_specs=[pl.BlockSpec(memory_space=pl.ANY)] * (4 + len(tables)),
        out_specs=vmem,
        scratch_shapes=[
            pltpu.SMEM(partner.shape, jnp.int32),
            pltpu.SMEM(geometry.shape, jnp.int32),
            pltpu.SMEM(band.shape, jnp.float32),
            pltpu.VMEM(x.shape, jnp.float32),
            *[pltpu.VMEM(t.shape, t.dtype) for t in tables],
            dma((4 + len(tables),)),
            pltpu.VMEM((2, views, vrows, LANES), jnp.float32),
            pltpu.VMEM((vrows * SLOT, LANES), jnp.float32),
            pltpu.VMEM((half - 1, strip, LANES), jnp.float32),
            pltpu.VMEM((n, strip, LANES), jnp.float32),
            pltpu.VMEM((NCOEF, 2, 2 * blocks, LANES), jnp.float32),
            pltpu.VMEM((nr, 8, LANES), jnp.float32),
            pltpu.VMEM((paired * 2 * PAD, 2 * LANES), jnp.float32),
            pltpu.VMEM((2, paired * blocks, 3 * LANES), jnp.bfloat16),
            pltpu.VMEM((2, paired * blocks, 3 * LANES), jnp.float32),
            dma((paired,)), dma((paired,)),
            dma((half - 1,)), dma((half - 1,)),
            dma((half - 1,)), dma((half - 1,)),
            dma((half,)), dma((half,)),
            dma((nr - 1,)), dma((nr - 1,)),
        ],
        compiler_params=pltpu.CompilerParams(
            collective_id=0, has_side_effects=True, vmem_limit_bytes=56 * 2**20),
        cost_estimate=pl.CostEstimate(flops=10**9, bytes_accessed=2 * 10**6, transcendentals=131072),
    )(partner, geometry, band, x, *[jnp.asarray(t) for t in tables])
    out = out.reshape(paired, TURNS, 2, LANES).transpose(0, 2, 1, 3)
    return out.reshape(paired, 2, WIDE)


def solution(mesh):
    in_specs = (P("views", "rows", None), P(), P())
    out_specs = P("views", "rows", None)
    n, nr = mesh.shape["views"], mesh.shape["rows"]
    return jax.shard_map(
        functools.partial(on_device, n, nr), mesh=mesh, in_specs=in_specs, out_specs=out_specs, check_vma=False
    )
```

```python
import functools
import math

import jax
import jax.numpy as jnp
import numpy as np
from jax import lax
from jax.experimental import pallas as pl
from jax.experimental.pallas import tpu as pltpu
from jax.sharding import PartitionSpec as P

GBAND = 4
WIDE = 7680
LANES = 128
TURNS = WIDE // LANES
PAD = 32
NCOEF = 2 * GBAND - 1
SLOT = 8

SHRINK_FLOOR = 1e-06
MESH = pl.DeviceIdType.MESH


def each(count, body):
    if count <= 16:
        for i in range(count):
            body(i)
    else:
        lax.fori_loop(0, count, lambda i, c: (body(i), c)[1], 0)


def split_np(table):
    hi = np.asarray(table, np.float32).astype(jnp.bfloat16)
    lo = (np.asarray(table, np.float64) - hi.astype(np.float64)).astype(jnp.bfloat16)
    return hi, lo


def split(x):
    hi = x.astype(jnp.bfloat16)
    lo = (x - hi.astype(jnp.float32)).astype(jnp.bfloat16)
    return hi, lo


def phase_table():
    i = np.arange(LANES)[:, None]
    j = np.arange(LANES)[None, :]
    parts = []
    for apart in (0, 1, -1):
        dist = np.abs(LANES * apart + j - i)
        parts.append(np.where(dist <= 126, np.exp2(-np.minimum(dist, 126).astype(np.float64)), 0.0))
    one = np.concatenate(parts, axis=1)
    return np.stack([one, one[::-1]]).astype(jnp.bfloat16)


def ramp_tables(left_blocks, right_start):
    k = np.arange(PAD)
    a = np.concatenate([np.arange(left_blocks), right_start + np.arange(left_blocks)])
    live = (k <= TURNS // 2)[:, None]
    ang = 2.0 * math.pi / TURNS * ((k[:, None] * a[None, :]) % TURNS)
    first = np.concatenate([np.where(live, np.cos(ang), 0), np.where(live, -np.sin(ang), 0)])
    fhi, flo = split_np(first)
    first = np.concatenate([fhi, fhi, flo], axis=1)
    b = np.arange(LANES)
    ang = 2.0 * math.pi / LANES * ((b[:, None] * b[None, :]) % LANES)
    c, s = np.cos(ang), np.sin(ang)
    fwd = split_np(np.block([[c, -s], [s, c]]))
    inv = split_np(np.block([[c, s], [-s, c]]))
    ang = 2.0 * math.pi / WIDE * ((k[:, None] * b[None, :]) % WIDE)
    twist = np.stack([np.cos(ang), np.sin(ang)]).astype(np.float32)
    freq = TURNS * b[None, :] + k[:, None]
    times = np.where((k == 0) | (k == TURNS // 2), 1.0, 2.0)[:, None]
    response = np.where(live, 2.0 * np.minimum(freq, WIDE - freq) / WIDE * times / WIDE, 0.0)
    a = np.arange(64)
    ang = 2.0 * math.pi / TURNS * ((a[:, None] * k[None, :]) % TURNS)
    last = np.concatenate([np.cos(ang), -np.sin(ang)], axis=1) * np.concatenate([live, live])[:, 0]
    lhi, llo = split_np(last)
    last = np.concatenate([lhi, lhi, llo], axis=1)
    return first, twist, np.stack(fwd), response.astype(np.float32), np.stack(inv), last


def band_tables(half_total):
    j = np.arange(half_total)[:, None]
    g = np.arange(GBAND)[None, :]
    ang = 2.0 * math.pi / half_total * ((j * g) % half_total)
    zero = np.zeros((half_total, 1))
    fwd = np.concatenate([np.cos(ang), -np.sin(ang[:, 1:]), zero], axis=1)
    dbl = np.where(g == 0, 1.0, 2.0)
    inv = np.concatenate([dbl * np.cos(ang), -2.0 * np.sin(ang[:, 1:]), zero], axis=1) / half_total
    return np.concatenate([fwd, inv], axis=1).reshape(-1).astype(np.float32)


def dot(a, b):
    return jnp.dot(a, b, preferred_element_type=jnp.float32)


def kernel(
    n, nr, views, blocks, rows_total,
    partner_hbm, geometry_hbm, band_hbm, x_hbm, phase_hbm, first_hbm, twist_hbm, fwd_hbm, resp_hbm, inv_hbm, last_hbm,
    out_ref,
    partner, geometry, band, x_ref, phase_ref, first_ref, twist_ref, fwd_ref, resp_ref, inv_ref, last_ref, ld_sem,
    st, cbuf, rsbuf, agbuf, full, pwbuf, pvbuf, lapbuf, mid, mv, z,
    ex_send, ex_recv, rs_send, rs_recv, ag_send, ag_recv, fw_send, fw_recv, pw_send, pw_recv, pv_send, pv_recv,
    lap_send, lap_recv,
):
    half = n // 2
    paired = views // 2
    me = lax.axis_index("views")
    my_row = lax.axis_index("rows")
    upper = me >= half
    up = jnp.where(upper, 1, 0)
    s = lax.rem(me, half)
    side = 1 - up
    other = lax.rem(me + half, n)
    strip = cbuf.shape[0] // half
    cols = blocks * LANES
    vrows = 2 * blocks

    barrier = pltpu.get_barrier_semaphore()

    def greet_view(d):
        pl.semaphore_signal(barrier, inc=1, device_id={"views": lax.rem(me + d + 1, n)}, device_id_type=MESH)

    def greet_row(d):
        pl.semaphore_signal(barrier, inc=1, device_id={"rows": lax.rem(my_row + d + 1, nr)}, device_id_type=MESH)

    each(n - 1, greet_view)
    each(nr - 1, greet_row)

    sources = (geometry_hbm, partner_hbm, x_hbm, phase_hbm, band_hbm, first_hbm, twist_hbm, fwd_hbm, resp_hbm, inv_hbm,
               last_hbm)
    targets = (geometry, partner, x_ref, phase_ref, band, first_ref, twist_ref, fwd_ref, resp_ref, inv_ref, last_ref)
    loads = [pltpu.make_async_copy(a, b, ld_sem.at[i]) for i, (a, b) in enumerate(zip(sources, targets))]
    for load in loads:
        load.start()
    for load in loads[:4]:
        load.wait()

    margins = [geometry[0, my_row * 2 + r] for r in range(2)]
    offsets = [geometry[1, my_row * 2 + r] for r in range(2)]
    move = [jnp.where(upper, cols - offsets[r], 2 * cols - WIDE - margins[r] - offsets[r]) for r in range(2)]
    whole = [move[r] // LANES for r in range(2)]
    rest = [move[r] - whole[r] * LANES for r in range(2)]
    ri = lax.broadcasted_iota(jnp.int32, (vrows, vrows), 0)
    ci = lax.broadcasted_iota(jnp.int32, (vrows, vrows), 1)
    second = ri >= blocks
    a_id = jnp.where(second, ri - blocks, ri)
    a_id = a_id - jnp.where(second, whole[1], whole[0])
    a_id = jnp.where(a_id < 0, a_id + blocks, a_id)
    a_id = jnp.where(upper, blocks - 1 - a_id, a_id)
    pick = (ci == 2 * a_id + jnp.where(second, 1, 0)).astype(jnp.float32).astype(jnp.bfloat16)

    rl = lax.broadcasted_iota(jnp.int32, (vrows, LANES), 0)
    lane = lax.broadcasted_iota(jnp.int32, (vrows, LANES), 1)
    sec = rl >= blocks
    t = jnp.where(sec, rl - blocks, rl) * LANES + lane + jnp.where(upper, 0, WIDE - cols)
    offs = jnp.where(sec, offsets[1], offsets[0])
    marg = jnp.where(sec, margins[1], margins[0])
    ramp = ((t + offs - cols + marg).astype(jnp.float32) + 0.5) / marg.astype(jnp.float32)
    w = jnp.minimum(jnp.maximum(ramp, 0.0), 1.0)
    weight = jnp.where(upper, 1.0 - w, w)
    lane_b = lax.broadcasted_iota(jnp.int32, (blocks, LANES), 1)

    half_total = views * half
    base = s * views
    r128 = lax.broadcasted_iota(jnp.int32, (LANES, LANES), 0)
    c128 = lax.broadcasted_iota(jnp.int32, (LANES, LANES), 1)
    one = phase_ref[up]
    phases = []
    for r in range(2):
        to = r128 + rest[r]
        to = jnp.where(to >= LANES, to - LANES, to)
        turn = (to == c128).astype(jnp.float32).astype(jnp.bfloat16)
        turned = [dot(one[:, p * LANES:(p + 1) * LANES], turn) for p in range(3)]
        turned = jnp.concatenate(turned, axis=1).astype(jnp.bfloat16)
        phases.append(jnp.concatenate([turned] * 3, axis=0))

    def place(start):
        for v in range(paired):
            i = start + v
            src = jnp.where(upper, partner[base + i] - half_total - base, i)
            x = x_ref[jnp.minimum(jnp.maximum(src, 0), views - 1)]
            hi = x.astype(jnp.bfloat16)
            left = x - hi.astype(jnp.float32)
            md = left.astype(jnp.bfloat16)
            lo = (left - md.astype(jnp.float32)).astype(jnp.bfloat16)
            moved = dot(pick, jnp.concatenate([hi, md, lo], axis=1)).astype(jnp.bfloat16)
            for r in range(2):
                mv[r, v * blocks:(v + 1) * blocks, :] = moved[r * blocks:(r + 1) * blocks]
        for r in range(2):
            z[r] = dot(mv[r], phases[r])
        for v in range(paired):
            lines = []
            for r in range(2):
                rows = slice(v * blocks, (v + 1) * blocks)
                y = (
                    z[r, rows, :LANES]
                    + pltpu.roll(z[r, rows, LANES:2 * LANES], 1, 0)
                    + pltpu.roll(z[r, rows, 2 * LANES:], blocks - 1, 0)
                )
                y = -jnp.log(y * (1.0 / 3.0))
                y = jnp.where(lane_b < rest[r], pltpu.roll(y, 1, 0), y)
                lines.append(y)
            st[side, start + v] = weight * jnp.concatenate(lines, axis=0)

    def ex_copy(v):
        i = (1 - up) * paired + v
        return pltpu.make_async_remote_copy(
            src_ref=st.at[side, i], dst_ref=st.at[side, i],
            send_sem=ex_send.at[v], recv_sem=ex_recv.at[v],
            device_id={"views": other}, device_id_type=MESH)

    place(0)
    place(paired)

    for load in loads[4:]:
        load.wait()
    for k in range(NCOEF):
        acc = None
        for i in range(views):
            term = band[(base + i) * 16 + k] * st[side, i]
            acc = term if acc is None else acc + term
        cbuf[pl.ds(k, vrows, stride=SLOT), :] = acc
    cbuf[pl.ds(NCOEF, vrows, stride=SLOT), :] = jnp.zeros((vrows, LANES), jnp.float32)

    pl.semaphore_wait(barrier, n + nr - 2)

    def rs_copy(d):
        to = lax.rem(s + d + 1, half)
        return pltpu.make_async_remote_copy(
            src_ref=cbuf.at[pl.ds(pl.multiple_of(to * strip, 8), strip)], dst_ref=rsbuf.at[d],
            send_sem=rs_send.at[d], recv_sem=rs_recv.at[d],
            device_id={"views": up * half + to}, device_id_type=MESH)

    lap = 2 * blocks - TURNS
    per = strip // SLOT
    piece = min(per, lap)
    pieces = [(r * blocks + q * piece, r * blocks + blocks - lap + q * piece)
              for r in range(2) for q in range(lap // piece)]

    def lap_copy(m, e):
        low, high = pieces[m]
        return pltpu.make_async_remote_copy(
            src_ref=cbuf.at[pl.ds(low * SLOT, piece * SLOT)], dst_ref=lapbuf.at[e],
            send_sem=lap_send.at[m], recv_sem=lap_recv.at[e],
            device_id={"views": half + high // per}, device_id_type=MESH)

    each(half - 1, lambda d: rs_copy(d).start())

    @pl.when(jnp.logical_not(upper))
    def _():
        for m in range(len(pieces)):
            lap_copy(m, me).start()

    for v in range(paired):
        ex_copy(v).start()
    agbuf[me] = cbuf[pl.ds(pl.multiple_of(s * strip, 8), strip), :]

    def rs_add(d):
        rs_copy(d).wait_recv()
        agbuf[me] = agbuf[me] + rsbuf[d]

    each(half - 1, rs_add)
    for m, (low, high) in enumerate(pieces):
        @pl.when(jnp.logical_and(upper, s == high // per))
        def _():
            at = pl.ds(high % per * SLOT, piece * SLOT)

            def lap_add(e):
                lap_copy(m, e).wait_recv()
                agbuf[me, at, :] = agbuf[me, at, :] + lapbuf[e]

            each(half, lap_add)

        @pl.when(jnp.logical_and(jnp.logical_not(upper), s == low // per))
        def _():
            agbuf[me, pl.ds(low % per * SLOT, piece * SLOT), :] = jnp.zeros((piece * SLOT, LANES), jnp.float32)

    par = lax.rem(me, 2)
    sibling = me + 1 - 2 * par

    def ag_copy(d, slot):
        return pltpu.make_async_remote_copy(
            src_ref=agbuf.at[slot], dst_ref=agbuf.at[slot],
            send_sem=ag_send.at[d], recv_sem=ag_recv.at[d],
            device_id={"views": lax.rem(me + 2 * d + 2, n)}, device_id_type=MESH)

    def fw_copy(d, slot):
        return pltpu.make_async_remote_copy(
            src_ref=agbuf.at[slot], dst_ref=agbuf.at[slot],
            send_sem=fw_send.at[d], recv_sem=fw_recv.at[d],
            device_id={"views": sibling}, device_id_type=MESH)

    def came(d):
        return lax.rem(me + n - 2 * d - 2, n)

    def came_sibling(d):
        return lax.rem(sibling + n - 2 * d - 2, n)

    def pw_copy(d):
        return pltpu.make_async_remote_copy(
            src_ref=pwbuf.at[0], dst_ref=pwbuf.at[d + 1],
            send_sem=pw_send.at[d], recv_sem=pw_recv.at[d],
            device_id={"rows": lax.rem(my_row + d + 1, nr)}, device_id_type=MESH)

    def pv_copy(d):
        return pltpu.make_async_remote_copy(
            src_ref=pvbuf.at[0], dst_ref=pvbuf.at[d + 1],
            send_sem=pv_send.at[d], recv_sem=pv_recv.at[d],
            device_id={"views": lax.rem(me + d + 1, n)}, device_id_type=MESH)

    each(half - 1, lambda d: ag_copy(d, me).start())
    fw_copy(half - 1, me).start()
    mine = agbuf[me]
    mine = mine * mine
    acc = mine[:SLOT]
    for q in range(1, per):
        acc = acc + mine[q * SLOT:(q + 1) * SLOT]
    pwbuf[0] = acc
    each(nr - 1, lambda d: pw_copy(d).start())
    each(half - 1, lambda d: rs_copy(d).wait_send())

    @pl.when(jnp.logical_not(upper))
    def _():
        for m in range(len(pieces)):
            lap_copy(m, me).wait_send()

    def forward(d):
        ag_copy(d, came(d)).wait_recv()
        fw_copy(d, came(d)).start()

    each(half - 1, forward)
    each(nr - 1, lambda d: pw_copy(d).wait_recv())
    acc = pwbuf[0]
    for d in range(nr - 1):
        acc = acc + pwbuf[d + 1]
    pvbuf[0] = acc
    each(n - 1, lambda d: pv_copy(d).start())
    fw_copy(half - 1, sibling).wait_recv()
    each(half - 1, lambda d: fw_copy(d, came_sibling(d)).wait_recv())
    each(half - 1, lambda d: ag_copy(d, me).wait_send())
    each(half - 1, lambda d: fw_copy(d, came(d)).wait_send())
    fw_copy(half - 1, me).wait_send()

    for k in range(NCOEF):
        sides = []
        for first_slot in (half, 0):
            got = [agbuf[first_slot + q, pl.ds(k, per, stride=SLOT), :] for q in range(half)]
            sides.append(jnp.concatenate(got, axis=0))
        for r in range(2):
            full[k, r] = jnp.concatenate([side_k[r * blocks:(r + 1) * blocks] for side_k in sides], axis=0)
    for v in range(paired):
        ex_copy(v).wait_send()
    for v in range(paired):
        i = up * paired + v
        pltpu.make_async_remote_copy(
            src_ref=st.at[1 - side, i], dst_ref=st.at[1 - side, i],
            send_sem=ex_send.at[v], recv_sem=ex_recv.at[v],
            device_id={"views": other}, device_id_type=MESH).wait_recv()
    each(n - 1, lambda d: pv_copy(d).wait_recv())
    total = pvbuf[0]
    if n <= 16:
        for d in range(n - 1):
            total = total + pvbuf[d + 1]
    else:
        total = lax.fori_loop(1, n, lambda d, c: c + pvbuf[d], total)
    total = jnp.sum(total, axis=1, keepdims=True)
    power = [total[g:g + 1] + (total[GBAND + g - 1:GBAND + g] if g else 0.0) for g in range(GBAND)]
    power = [p / (rows_total * WIDE) + SHRINK_FLOOR for p in power]
    for r in range(2):
        for g in range(GBAND):
            re = full[g, r]
            mag = re * re
            if g:
                im = full[GBAND + g - 1, r]
                mag = mag + im * im
            factor = (1.0 - (g / GBAND) ** 2) * mag / (mag + power[g])
            full[g, r] = factor * re
            if g:
                full[GBAND + g - 1, r] = factor * im
    each(nr - 1, lambda d: pw_copy(d).wait_send())
    each(n - 1, lambda d: pv_copy(d).wait_send())

    cos, sin = twist_ref[0], twist_ref[1]
    first = first_ref[...]
    for v in range(paired):
        i = up * paired + v
        lines = []
        for r in range(2):
            line = jnp.concatenate([st[0, i, r * blocks:(r + 1) * blocks],
                                    st[1, i, r * blocks:(r + 1) * blocks]], axis=0)
            for k in range(NCOEF):
                line = line - band[(base + i) * 16 + 8 + k] * full[k, r]
            lines.append(line)
        hi, lo = split(jnp.concatenate(lines, axis=1))
        step = dot(first, jnp.concatenate([hi, lo, hi], axis=0))
        for r in range(2):
            re = step[:PAD, r * LANES:(r + 1) * LANES]
            im = step[PAD:, r * LANES:(r + 1) * LANES]
            at = (2 * v + r) * PAD
            mid[at:at + PAD, :LANES] = re * cos + im * sin
            mid[at:at + PAD, LANES:] = im * cos - re * sin

    hi, lo = split(mid[...])
    spec = dot(hi, fwd_ref[0]) + dot(lo, fwd_ref[0]) + dot(hi, fwd_ref[1])
    resp = resp_ref[...]
    resp = jnp.concatenate([resp, resp], axis=1)
    resp = jnp.concatenate([resp] * (2 * paired), axis=0)
    hi, lo = split(spec * resp)
    mid[...] = dot(hi, inv_ref[0]) + dot(lo, inv_ref[0]) + dot(hi, inv_ref[1])

    last = last_ref[...]
    for v in range(paired):
        res, ims = [], []
        for r in range(2):
            at = (2 * v + r) * PAD
            re = mid[at:at + PAD, :LANES]
            im = mid[at:at + PAD, LANES:]
            res.append(re * cos - im * sin)
            ims.append(im * cos + re * sin)
        both = jnp.concatenate([jnp.concatenate(res, axis=1), jnp.concatenate(ims, axis=1)], axis=0)
        hi, lo = split(both)
        y = dot(last, jnp.concatenate([hi, lo, hi], axis=0))
        for r in range(2):
            out_ref[pl.ds(v * 2 * TURNS + r, TURNS, stride=2), :] = y[:TURNS, r * LANES:(r + 1) * LANES]


def on_device(n, nr, projections, partner, geometry):
    views, row_dev, cols = projections.shape
    assert row_dev == 2
    blocks = cols // LANES
    half = n // 2
    vrows = 2 * blocks
    strip = vrows * SLOT // half
    lap = 2 * blocks - TURNS
    piece = min(strip // SLOT, lap)
    x = projections.reshape(views, row_dev, blocks, LANES).transpose(0, 2, 1, 3).reshape(views, vrows, LANES)
    tables = (phase_table(),) + ramp_tables(blocks, TURNS - blocks)
    band = jnp.asarray(band_tables(views * half))
    vmem = pl.BlockSpec(memory_space=pltpu.VMEM)
    paired = views // 2
    dma = pltpu.SemaphoreType.DMA
    out = pl.pallas_call(
        functools.partial(kernel, n, nr, views, blocks, row_dev * nr),
        out_shape=jax.ShapeDtypeStruct((paired * 2 * TURNS, LANES), jnp.float32),
        in_specs=[pl.BlockSpec(memory_space=pl.ANY)] * (4 + len(tables)),
        out_specs=vmem,
        scratch_shapes=[
            pltpu.SMEM(partner.shape, jnp.int32),
            pltpu.SMEM(geometry.shape, jnp.int32),
            pltpu.SMEM(band.shape, jnp.float32),
            pltpu.VMEM(x.shape, jnp.float32),
            *[pltpu.VMEM(t.shape, t.dtype) for t in tables],
            dma((4 + len(tables),)),
            pltpu.VMEM((2, views, vrows, LANES), jnp.float32),
            pltpu.VMEM((vrows * SLOT, LANES), jnp.float32),
            pltpu.VMEM((half - 1, strip, LANES), jnp.float32),
            pltpu.VMEM((n, strip, LANES), jnp.float32),
            pltpu.VMEM((NCOEF, 2, 2 * blocks, LANES), jnp.float32),
            pltpu.VMEM((nr, SLOT, LANES), jnp.float32),
            pltpu.VMEM((n, SLOT, LANES), jnp.float32),
            pltpu.VMEM((half, piece * SLOT, LANES), jnp.float32),
            pltpu.VMEM((paired * 2 * PAD, 2 * LANES), jnp.float32),
            pltpu.VMEM((2, paired * blocks, 3 * LANES), jnp.bfloat16),
            pltpu.VMEM((2, paired * blocks, 3 * LANES), jnp.float32),
            dma((paired,)), dma((paired,)),
            dma((half - 1,)), dma((half - 1,)),
            dma((half - 1,)), dma((half - 1,)),
            dma((half,)), dma((half,)),
            dma((nr - 1,)), dma((nr - 1,)),
            dma((n - 1,)), dma((n - 1,)),
            dma((2 * (lap // piece),)), dma((half,)),
        ],
        compiler_params=pltpu.CompilerParams(
            collective_id=0, has_side_effects=True, vmem_limit_bytes=56 * 2**20),
        cost_estimate=pl.CostEstimate(flops=10**9, bytes_accessed=2 * 10**6, transcendentals=131072),
    )(partner, geometry, band, x, *[jnp.asarray(t) for t in tables])
    out = out.reshape(paired, TURNS, 2, LANES).transpose(0, 2, 1, 3)
    return out.reshape(paired, 2, WIDE)


def solution(mesh):
    in_specs = (P("views", "rows", None), P(), P())
    out_specs = P("views", "rows", None)
    n, nr = mesh.shape["views"], mesh.shape["rows"]
    return jax.shard_map(
        functools.partial(on_device, n, nr), mesh=mesh, in_specs=in_specs, out_specs=out_specs, check_vma=False
    )
```

```python
import functools
import math

import jax
import jax.numpy as jnp
import numpy as np
from jax import lax
from jax.experimental import pallas as pl
from jax.experimental.pallas import tpu as pltpu
from jax.sharding import PartitionSpec as P

GBAND = 4
WIDE = 7680
LANES = 128
TURNS = WIDE // LANES
PAD = 32
NCOEF = 2 * GBAND - 1
SLOT = 8

SHRINK_FLOOR = 1e-06
MESH = pl.DeviceIdType.MESH


def each(count, body):
    if count <= 32:
        for i in range(count):
            body(i)
    else:
        lax.fori_loop(0, count, lambda i, c: (body(i), c)[1], 0)


def split_np(table):
    hi = np.asarray(table, np.float32).astype(jnp.bfloat16)
    lo = (np.asarray(table, np.float64) - hi.astype(np.float64)).astype(jnp.bfloat16)
    return hi, lo


def split(x):
    hi = x.astype(jnp.bfloat16)
    lo = (x - hi.astype(jnp.float32)).astype(jnp.bfloat16)
    return hi, lo


def phase_table():
    i = np.arange(LANES)[:, None]
    j = np.arange(LANES)[None, :]
    parts = []
    for apart in (0, 1, -1):
        dist = np.abs(LANES * apart + j - i)
        parts.append(np.where(dist <= 126, np.exp2(-np.minimum(dist, 126).astype(np.float64)), 0.0))
    one = np.concatenate(parts, axis=1)
    return np.stack([one, one[::-1]]).astype(jnp.bfloat16)


def ramp_tables(left_blocks, right_start):
    k = np.arange(PAD)
    a = np.concatenate([np.arange(left_blocks), right_start + np.arange(left_blocks)])
    live = (k <= TURNS // 2)[:, None]
    ang = 2.0 * math.pi / TURNS * ((k[:, None] * a[None, :]) % TURNS)
    first = np.concatenate([np.where(live, np.cos(ang), 0), np.where(live, -np.sin(ang), 0)])
    fhi, flo = split_np(first)
    first = np.concatenate([fhi, fhi, flo], axis=1)
    b = np.arange(LANES)
    ang = 2.0 * math.pi / LANES * ((b[:, None] * b[None, :]) % LANES)
    c, s = np.cos(ang), np.sin(ang)
    fwd = split_np(np.block([[c, -s], [s, c]]))
    inv = split_np(np.block([[c, s], [-s, c]]))
    ang = 2.0 * math.pi / WIDE * ((k[:, None] * b[None, :]) % WIDE)
    twist = np.stack([np.cos(ang), np.sin(ang)]).astype(np.float32)
    freq = TURNS * b[None, :] + k[:, None]
    times = np.where((k == 0) | (k == TURNS // 2), 1.0, 2.0)[:, None]
    response = np.where(live, 2.0 * np.minimum(freq, WIDE - freq) / WIDE * times / WIDE, 0.0)
    a = np.arange(64)
    ang = 2.0 * math.pi / TURNS * ((a[:, None] * k[None, :]) % TURNS)
    last = np.concatenate([np.cos(ang), -np.sin(ang)], axis=1) * np.concatenate([live, live])[:, 0]
    lhi, llo = split_np(last)
    last = np.concatenate([lhi, lhi, llo], axis=1)
    return first, twist, np.stack(fwd), response.astype(np.float32), np.stack(inv), last


def band_tables(half_total):
    j = np.arange(half_total)[:, None]
    g = np.arange(GBAND)[None, :]
    ang = 2.0 * math.pi / half_total * ((j * g) % half_total)
    zero = np.zeros((half_total, 1))
    fwd = np.concatenate([np.cos(ang), -np.sin(ang[:, 1:]), zero], axis=1)
    dbl = np.where(g == 0, 1.0, 2.0)
    inv = np.concatenate([dbl * np.cos(ang), -2.0 * np.sin(ang[:, 1:]), zero], axis=1) / half_total
    return np.concatenate([fwd, inv], axis=1).reshape(-1).astype(np.float32)


def dot(a, b):
    return jnp.dot(a, b, preferred_element_type=jnp.float32)


def kernel(
    n, nr, views, blocks, rows_total,
    partner_hbm, geometry_hbm, band_hbm, x_hbm, phase_hbm, first_hbm, twist_hbm, fwd_hbm, resp_hbm, inv_hbm, last_hbm,
    out_ref,
    partner, geometry, band, x_ref, phase_ref, first_ref, twist_ref, fwd_ref, resp_ref, inv_ref, last_ref, ld_sem,
    st, cbuf, rsbuf, agbuf, full, pvbuf, lapbuf, mid, mv, z,
    ex_send, ex_recv, rs_send, rs_recv, ag_send, ag_recv, fw_send, fw_recv, pv_send, pv_recv,
    lap_send, lap_recv,
):
    half = n // 2
    paired = views // 2
    me = lax.axis_index("views")
    my_row = lax.axis_index("rows")
    upper = me >= half
    up = jnp.where(upper, 1, 0)
    s = lax.rem(me, half)
    side = 1 - up
    other = lax.rem(me + half, n)
    strip = cbuf.shape[0] // half
    cols = blocks * LANES
    vrows = 2 * blocks

    barrier = pltpu.get_barrier_semaphore()

    def greet(d):
        to = lax.rem(my_row * n + me + d + 1, n * nr)
        pl.semaphore_signal(barrier, inc=1, device_id={"views": lax.rem(to, n), "rows": to // n}, device_id_type=MESH)

    each(n * nr - 1, greet)

    sources = (geometry_hbm, partner_hbm, x_hbm, phase_hbm, band_hbm, first_hbm, twist_hbm, fwd_hbm, resp_hbm, inv_hbm,
               last_hbm)
    targets = (geometry, partner, x_ref, phase_ref, band, first_ref, twist_ref, fwd_ref, resp_ref, inv_ref, last_ref)
    loads = [pltpu.make_async_copy(a, b, ld_sem.at[i]) for i, (a, b) in enumerate(zip(sources, targets))]
    for load in loads:
        load.start()
    for load in loads[:4]:
        load.wait()

    margins = [geometry[0, my_row * 2 + r] for r in range(2)]
    offsets = [geometry[1, my_row * 2 + r] for r in range(2)]
    move = [jnp.where(upper, cols - offsets[r], 2 * cols - WIDE - margins[r] - offsets[r]) for r in range(2)]
    whole = [move[r] // LANES for r in range(2)]
    rest = [move[r] - whole[r] * LANES for r in range(2)]
    ri = lax.broadcasted_iota(jnp.int32, (vrows, vrows), 0)
    ci = lax.broadcasted_iota(jnp.int32, (vrows, vrows), 1)
    second = ri >= blocks
    a_id = jnp.where(second, ri - blocks, ri)
    a_id = a_id - jnp.where(second, whole[1], whole[0])
    a_id = jnp.where(a_id < 0, a_id + blocks, a_id)
    a_id = jnp.where(upper, blocks - 1 - a_id, a_id)
    pick = (ci == 2 * a_id + jnp.where(second, 1, 0)).astype(jnp.float32).astype(jnp.bfloat16)

    rl = lax.broadcasted_iota(jnp.int32, (vrows, LANES), 0)
    lane = lax.broadcasted_iota(jnp.int32, (vrows, LANES), 1)
    sec = rl >= blocks
    t = jnp.where(sec, rl - blocks, rl) * LANES + lane + jnp.where(upper, 0, WIDE - cols)
    offs = jnp.where(sec, offsets[1], offsets[0])
    marg = jnp.where(sec, margins[1], margins[0])
    ramp = ((t + offs - cols + marg).astype(jnp.float32) + 0.5) / marg.astype(jnp.float32)
    w = jnp.minimum(jnp.maximum(ramp, 0.0), 1.0)
    weight = jnp.where(upper, 1.0 - w, w)
    lane_b = lax.broadcasted_iota(jnp.int32, (blocks, LANES), 1)

    half_total = views * half
    base = s * views
    r128 = lax.broadcasted_iota(jnp.int32, (LANES, LANES), 0)
    c128 = lax.broadcasted_iota(jnp.int32, (LANES, LANES), 1)
    one = phase_ref[up]
    phases = []
    for r in range(2):
        to = r128 + rest[r]
        to = jnp.where(to >= LANES, to - LANES, to)
        turn = (to == c128).astype(jnp.float32).astype(jnp.bfloat16)
        turned = [dot(one[:, p * LANES:(p + 1) * LANES], turn) for p in range(3)]
        turned = jnp.concatenate(turned, axis=1).astype(jnp.bfloat16)
        phases.append(jnp.concatenate([turned] * 3, axis=0))

    def place(start):
        for v in range(paired):
            i = start + v
            src = jnp.where(upper, partner[base + i] - half_total - base, i)
            x = x_ref[jnp.minimum(jnp.maximum(src, 0), views - 1)]
            hi = x.astype(jnp.bfloat16)
            left = x - hi.astype(jnp.float32)
            md = left.astype(jnp.bfloat16)
            lo = (left - md.astype(jnp.float32)).astype(jnp.bfloat16)
            moved = dot(pick, jnp.concatenate([hi, md, lo], axis=1)).astype(jnp.bfloat16)
            for r in range(2):
                mv[r, v * blocks:(v + 1) * blocks, :] = moved[r * blocks:(r + 1) * blocks]
        for r in range(2):
            z[r] = dot(mv[r], phases[r])
        for v in range(paired):
            lines = []
            for r in range(2):
                rows = slice(v * blocks, (v + 1) * blocks)
                y = (
                    z[r, rows, :LANES]
                    + pltpu.roll(z[r, rows, LANES:2 * LANES], 1, 0)
                    + pltpu.roll(z[r, rows, 2 * LANES:], blocks - 1, 0)
                )
                y = -jnp.log(y * (1.0 / 3.0))
                y = jnp.where(lane_b < rest[r], pltpu.roll(y, 1, 0), y)
                lines.append(y)
            st[side, start + v] = weight * jnp.concatenate(lines, axis=0)

    def ex_copy(v):
        i = (1 - up) * paired + v
        return pltpu.make_async_remote_copy(
            src_ref=st.at[side, i], dst_ref=st.at[side, i],
            send_sem=ex_send.at[v], recv_sem=ex_recv.at[v],
            device_id={"views": other}, device_id_type=MESH)

    place(0)
    place(paired)

    for load in loads[4:]:
        load.wait()
    for k in range(NCOEF):
        acc = None
        for i in range(views):
            term = band[(base + i) * 16 + k] * st[side, i]
            acc = term if acc is None else acc + term
        cbuf[pl.ds(k, vrows, stride=SLOT), :] = acc
    cbuf[pl.ds(NCOEF, vrows, stride=SLOT), :] = jnp.zeros((vrows, LANES), jnp.float32)

    pl.semaphore_wait(barrier, n * nr - 1)

    def rs_copy(d):
        to = lax.rem(s + d + 1, half)
        return pltpu.make_async_remote_copy(
            src_ref=cbuf.at[pl.ds(pl.multiple_of(to * strip, 8), strip)], dst_ref=rsbuf.at[d],
            send_sem=rs_send.at[d], recv_sem=rs_recv.at[d],
            device_id={"views": up * half + to}, device_id_type=MESH)

    lap = 2 * blocks - TURNS
    per = strip // SLOT
    piece = min(per, lap)
    pieces = [(r * blocks + q * piece, r * blocks + blocks - lap + q * piece)
              for r in range(2) for q in range(lap // piece)]

    def lap_copy(m, e):
        low, high = pieces[m]
        return pltpu.make_async_remote_copy(
            src_ref=cbuf.at[pl.ds(low * SLOT, piece * SLOT)], dst_ref=lapbuf.at[e],
            send_sem=lap_send.at[m], recv_sem=lap_recv.at[e],
            device_id={"views": half + high // per}, device_id_type=MESH)

    each(half - 1, lambda d: rs_copy(d).start())

    @pl.when(jnp.logical_not(upper))
    def _():
        for m in range(len(pieces)):
            lap_copy(m, me).start()

    for v in range(paired):
        ex_copy(v).start()
    agbuf[me] = cbuf[pl.ds(pl.multiple_of(s * strip, 8), strip), :]

    def rs_add(d):
        rs_copy(d).wait_recv()
        agbuf[me] = agbuf[me] + rsbuf[d]

    each(half - 1, rs_add)
    for m, (low, high) in enumerate(pieces):
        @pl.when(jnp.logical_and(upper, s == high // per))
        def _():
            at = pl.ds(high % per * SLOT, piece * SLOT)

            def lap_add(e):
                lap_copy(m, e).wait_recv()
                agbuf[me, at, :] = agbuf[me, at, :] + lapbuf[e]

            each(half, lap_add)

        @pl.when(jnp.logical_and(jnp.logical_not(upper), s == low // per))
        def _():
            agbuf[me, pl.ds(low % per * SLOT, piece * SLOT), :] = jnp.zeros((piece * SLOT, LANES), jnp.float32)

    par = lax.rem(me, 2)
    sibling = me + 1 - 2 * par

    def ag_copy(d, slot):
        return pltpu.make_async_remote_copy(
            src_ref=agbuf.at[slot], dst_ref=agbuf.at[slot],
            send_sem=ag_send.at[d], recv_sem=ag_recv.at[d],
            device_id={"views": lax.rem(me + 2 * d + 2, n)}, device_id_type=MESH)

    def fw_copy(d, slot):
        return pltpu.make_async_remote_copy(
            src_ref=agbuf.at[slot], dst_ref=agbuf.at[slot],
            send_sem=fw_send.at[d], recv_sem=fw_recv.at[d],
            device_id={"views": sibling}, device_id_type=MESH)

    def came(d):
        return lax.rem(me + n - 2 * d - 2, n)

    def came_sibling(d):
        return lax.rem(sibling + n - 2 * d - 2, n)

    everyone = n * nr
    place_id = my_row * n + me

    def pv_copy(d):
        to = lax.rem(place_id + d + 1, everyone)
        return pltpu.make_async_remote_copy(
            src_ref=pvbuf.at[0], dst_ref=pvbuf.at[d + 1],
            send_sem=pv_send.at[d], recv_sem=pv_recv.at[d],
            device_id={"views": lax.rem(to, n), "rows": to // n}, device_id_type=MESH)

    each(half - 1, lambda d: ag_copy(d, me).start())
    fw_copy(half - 1, me).start()
    mine = agbuf[me]
    mine = mine * mine
    acc = mine[:SLOT]
    for q in range(1, per):
        acc = acc + mine[q * SLOT:(q + 1) * SLOT]
    pvbuf[0] = acc
    each(everyone - 1, lambda d: pv_copy(d).start())
    each(half - 1, lambda d: rs_copy(d).wait_send())

    @pl.when(jnp.logical_not(upper))
    def _():
        for m in range(len(pieces)):
            lap_copy(m, me).wait_send()

    def forward(d):
        ag_copy(d, came(d)).wait_recv()
        fw_copy(d, came(d)).start()

    each(half - 1, forward)
    fw_copy(half - 1, sibling).wait_recv()
    each(half - 1, lambda d: fw_copy(d, came_sibling(d)).wait_recv())
    each(half - 1, lambda d: ag_copy(d, me).wait_send())
    each(half - 1, lambda d: fw_copy(d, came(d)).wait_send())
    fw_copy(half - 1, me).wait_send()

    for k in range(NCOEF):
        sides = []
        for first_slot in (half, 0):
            got = [agbuf[first_slot + q, pl.ds(k, per, stride=SLOT), :] for q in range(half)]
            sides.append(jnp.concatenate(got, axis=0))
        for r in range(2):
            full[k, r] = jnp.concatenate([side_k[r * blocks:(r + 1) * blocks] for side_k in sides], axis=0)
    for v in range(paired):
        ex_copy(v).wait_send()
    for v in range(paired):
        i = up * paired + v
        pltpu.make_async_remote_copy(
            src_ref=st.at[1 - side, i], dst_ref=st.at[1 - side, i],
            send_sem=ex_send.at[v], recv_sem=ex_recv.at[v],
            device_id={"views": other}, device_id_type=MESH).wait_recv()
    each(everyone - 1, lambda d: pv_copy(d).wait_recv())
    total = lax.fori_loop(1, everyone, lambda d, c: c + pvbuf[d], pvbuf[0], unroll=everyone <= 32)
    total = jnp.sum(total, axis=1, keepdims=True)
    power = [total[g:g + 1] + (total[GBAND + g - 1:GBAND + g] if g else 0.0) for g in range(GBAND)]
    power = [p / (rows_total * WIDE) + SHRINK_FLOOR for p in power]
    for r in range(2):
        for g in range(GBAND):
            re = full[g, r]
            mag = re * re
            if g:
                im = full[GBAND + g - 1, r]
                mag = mag + im * im
            factor = (1.0 - (g / GBAND) ** 2) * mag / (mag + power[g])
            full[g, r] = factor * re
            if g:
                full[GBAND + g - 1, r] = factor * im
    each(everyone - 1, lambda d: pv_copy(d).wait_send())

    cos, sin = twist_ref[0], twist_ref[1]
    first = first_ref[...]
    for v in range(paired):
        i = up * paired + v
        lines = []
        for r in range(2):
            line = jnp.concatenate([st[0, i, r * blocks:(r + 1) * blocks],
                                    st[1, i, r * blocks:(r + 1) * blocks]], axis=0)
            for k in range(NCOEF):
                line = line - band[(base + i) * 16 + 8 + k] * full[k, r]
            lines.append(line)
        hi, lo = split(jnp.concatenate(lines, axis=1))
        step = dot(first, jnp.concatenate([hi, lo, hi], axis=0))
        for r in range(2):
            re = step[:PAD, r * LANES:(r + 1) * LANES]
            im = step[PAD:, r * LANES:(r + 1) * LANES]
            at = (2 * v + r) * PAD
            mid[at:at + PAD, :LANES] = re * cos + im * sin
            mid[at:at + PAD, LANES:] = im * cos - re * sin

    hi, lo = split(mid[...])
    spec = dot(hi, fwd_ref[0]) + dot(lo, fwd_ref[0]) + dot(hi, fwd_ref[1])
    resp = resp_ref[...]
    resp = jnp.concatenate([resp, resp], axis=1)
    resp = jnp.concatenate([resp] * (2 * paired), axis=0)
    hi, lo = split(spec * resp)
    mid[...] = dot(hi, inv_ref[0]) + dot(lo, inv_ref[0]) + dot(hi, inv_ref[1])

    last = last_ref[...]
    for v in range(paired):
        res, ims = [], []
        for r in range(2):
            at = (2 * v + r) * PAD
            re = mid[at:at + PAD, :LANES]
            im = mid[at:at + PAD, LANES:]
            res.append(re * cos - im * sin)
            ims.append(im * cos + re * sin)
        both = jnp.concatenate([jnp.concatenate(res, axis=1), jnp.concatenate(ims, axis=1)], axis=0)
        hi, lo = split(both)
        y = dot(last, jnp.concatenate([hi, lo, hi], axis=0))
        for r in range(2):
            out_ref[pl.ds(v * 2 * TURNS + r, TURNS, stride=2), :] = y[:TURNS, r * LANES:(r + 1) * LANES]


def on_device(n, nr, projections, partner, geometry):
    views, row_dev, cols = projections.shape
    assert row_dev == 2
    blocks = cols // LANES
    half = n // 2
    vrows = 2 * blocks
    strip = vrows * SLOT // half
    lap = 2 * blocks - TURNS
    piece = min(strip // SLOT, lap)
    x = projections.reshape(views, row_dev, blocks, LANES).transpose(0, 2, 1, 3).reshape(views, vrows, LANES)
    tables = (phase_table(),) + ramp_tables(blocks, TURNS - blocks)
    band = jnp.asarray(band_tables(views * half))
    vmem = pl.BlockSpec(memory_space=pltpu.VMEM)
    paired = views // 2
    dma = pltpu.SemaphoreType.DMA
    out = pl.pallas_call(
        functools.partial(kernel, n, nr, views, blocks, row_dev * nr),
        out_shape=jax.ShapeDtypeStruct((paired * 2 * TURNS, LANES), jnp.float32),
        in_specs=[pl.BlockSpec(memory_space=pl.ANY)] * (4 + len(tables)),
        out_specs=vmem,
        scratch_shapes=[
            pltpu.SMEM(partner.shape, jnp.int32),
            pltpu.SMEM(geometry.shape, jnp.int32),
            pltpu.SMEM(band.shape, jnp.float32),
            pltpu.VMEM(x.shape, jnp.float32),
            *[pltpu.VMEM(t.shape, t.dtype) for t in tables],
            dma((4 + len(tables),)),
            pltpu.VMEM((2, views, vrows, LANES), jnp.float32),
            pltpu.VMEM((vrows * SLOT, LANES), jnp.float32),
            pltpu.VMEM((half - 1, strip, LANES), jnp.float32),
            pltpu.VMEM((n, strip, LANES), jnp.float32),
            pltpu.VMEM((NCOEF, 2, 2 * blocks, LANES), jnp.float32),
            pltpu.VMEM((n * nr, SLOT, LANES), jnp.float32),
            pltpu.VMEM((half, piece * SLOT, LANES), jnp.float32),
            pltpu.VMEM((paired * 2 * PAD, 2 * LANES), jnp.float32),
            pltpu.VMEM((2, paired * blocks, 3 * LANES), jnp.bfloat16),
            pltpu.VMEM((2, paired * blocks, 3 * LANES), jnp.float32),
            dma((paired,)), dma((paired,)),
            dma((half - 1,)), dma((half - 1,)),
            dma((half - 1,)), dma((half - 1,)),
            dma((half,)), dma((half,)),
            dma((n * nr - 1,)), dma((n * nr - 1,)),
            dma((2 * (lap // piece),)), dma((half,)),
        ],
        compiler_params=pltpu.CompilerParams(
            collective_id=0, has_side_effects=True, vmem_limit_bytes=56 * 2**20),
        cost_estimate=pl.CostEstimate(flops=10**9, bytes_accessed=2 * 10**6, transcendentals=131072),
    )(partner, geometry, band, x, *[jnp.asarray(t) for t in tables])
    out = out.reshape(paired, TURNS, 2, LANES).transpose(0, 2, 1, 3)
    return out.reshape(paired, 2, WIDE)


def solution(mesh):
    in_specs = (P("views", "rows", None), P(), P())
    out_specs = P("views", "rows", None)
    n, nr = mesh.shape["views"], mesh.shape["rows"]
    return jax.shard_map(
        functools.partial(on_device, n, nr), mesh=mesh, in_specs=in_specs, out_specs=out_specs, check_vma=False
    )
```

```python
import functools
import math

import jax
import jax.numpy as jnp
import numpy as np
from jax import lax
from jax.experimental import pallas as pl
from jax.experimental.pallas import tpu as pltpu
from jax.experimental.layout import Layout, with_layout_constraint
from jax.sharding import PartitionSpec as P

GBAND = 4
WIDE = 7680
LANES = 128
TURNS = WIDE // LANES
PAD = 32
NCOEF = 2 * GBAND - 1
SLOT = 8

SHRINK_FLOOR = 1e-06
MESH = pl.DeviceIdType.MESH


def each(count, body):
    if count <= 16:
        for i in range(count):
            body(i)
    else:
        lax.fori_loop(0, count, lambda i, c: (body(i), c)[1], 0)


def split_np(table):
    hi = np.asarray(table, np.float32).astype(jnp.bfloat16)
    lo = (np.asarray(table, np.float64) - hi.astype(np.float64)).astype(jnp.bfloat16)
    return hi, lo


def split(x):
    hi = x.astype(jnp.bfloat16)
    lo = (x - hi.astype(jnp.float32)).astype(jnp.bfloat16)
    return hi, lo


def phase_table():
    i = np.arange(LANES)[:, None]
    j = np.arange(LANES)[None, :]
    parts = []
    for apart in (0, 1, -1):
        dist = np.abs(LANES * apart + j - i)
        parts.append(np.where(dist <= 126, np.exp2(-np.minimum(dist, 126).astype(np.float64)), 0.0))
    one = np.concatenate(parts, axis=1)
    return np.stack([one, one[::-1]]).astype(jnp.bfloat16)


def ramp_tables(left_blocks, right_start):
    k = np.arange(PAD)
    a = np.concatenate([np.arange(left_blocks), right_start + np.arange(left_blocks)])
    live = (k <= TURNS // 2)[:, None]
    ang = 2.0 * math.pi / TURNS * ((k[:, None] * a[None, :]) % TURNS)
    first = np.concatenate([np.where(live, np.cos(ang), 0), np.where(live, -np.sin(ang), 0)])
    fhi, flo = split_np(first)
    first = np.concatenate([fhi, fhi, flo], axis=1)
    b = np.arange(LANES)
    ang = 2.0 * math.pi / LANES * ((b[:, None] * b[None, :]) % LANES)
    c, s = np.cos(ang), np.sin(ang)
    fwd = split_np(np.block([[c, -s], [s, c]]))
    inv = split_np(np.block([[c, s], [-s, c]]))
    ang = 2.0 * math.pi / WIDE * ((k[:, None] * b[None, :]) % WIDE)
    twist = np.stack([np.cos(ang), np.sin(ang)]).astype(np.float32)
    freq = TURNS * b[None, :] + k[:, None]
    times = np.where((k == 0) | (k == TURNS // 2), 1.0, 2.0)[:, None]
    response = np.where(live, 2.0 * np.minimum(freq, WIDE - freq) / WIDE * times / WIDE, 0.0)
    a = np.arange(64)
    ang = 2.0 * math.pi / TURNS * ((a[:, None] * k[None, :]) % TURNS)
    last = np.concatenate([np.cos(ang), -np.sin(ang)], axis=1) * np.concatenate([live, live])[:, 0]
    lhi, llo = split_np(last)
    last = np.concatenate([lhi, lhi, llo], axis=1)
    return first, twist, np.stack(fwd), response.astype(np.float32), np.stack(inv), last


def band_tables(half_total):
    j = np.arange(half_total)[:, None]
    g = np.arange(GBAND)[None, :]
    ang = 2.0 * math.pi / half_total * ((j * g) % half_total)
    zero = np.zeros((half_total, 1))
    fwd = np.concatenate([np.cos(ang), -np.sin(ang[:, 1:]), zero], axis=1)
    dbl = np.where(g == 0, 1.0, 2.0)
    inv = np.concatenate([dbl * np.cos(ang), -2.0 * np.sin(ang[:, 1:]), zero], axis=1) / half_total
    return np.concatenate([fwd, inv], axis=1).reshape(-1).astype(np.float32)


def dot(a, b):
    return jnp.dot(a, b, preferred_element_type=jnp.float32)


def kernel(
    n, nr, views, blocks, rows_total,
    partner_hbm, geometry_hbm, band_hbm, x_hbm, phase_hbm, first_hbm, twist_hbm, fwd_hbm, resp_hbm, inv_hbm, last_hbm,
    out_ref,
    partner, geometry, band, x_ref, phase_ref, first_ref, twist_ref, fwd_ref, resp_ref, inv_ref, last_ref, ld_sem,
    st, cbuf, rsbuf, agbuf, full, pwbuf, pvbuf, lapbuf, mid, mv, z,
    ex_send, ex_recv, rs_send, rs_recv, ag_send, ag_recv, fw_send, fw_recv, pw_send, pw_recv, pv_send, pv_recv,
    lap_send, lap_recv,
):
    half = n // 2
    paired = views // 2
    me = lax.axis_index("views")
    my_row = lax.axis_index("rows")
    upper = me >= half
    up = jnp.where(upper, 1, 0)
    s = lax.rem(me, half)
    side = 1 - up
    other = lax.rem(me + half, n)
    strip = cbuf.shape[0] // half
    cols = blocks * LANES
    vrows = 2 * blocks

    barrier = pltpu.get_barrier_semaphore()

    def greet_view(d):
        pl.semaphore_signal(barrier, inc=1, device_id={"views": lax.rem(me + d + 1, n)}, device_id_type=MESH)

    def greet_row(d):
        pl.semaphore_signal(barrier, inc=1, device_id={"rows": lax.rem(my_row + d + 1, nr)}, device_id_type=MESH)

    each(n - 1, greet_view)
    each(nr - 1, greet_row)

    sources = (geometry_hbm, partner_hbm, x_hbm, phase_hbm, band_hbm, first_hbm, twist_hbm, fwd_hbm, resp_hbm, inv_hbm,
               last_hbm)
    targets = (geometry, partner, x_ref, phase_ref, band, first_ref, twist_ref, fwd_ref, resp_ref, inv_ref, last_ref)
    loads = [pltpu.make_async_copy(a, b, ld_sem.at[i]) for i, (a, b) in enumerate(zip(sources, targets))]
    for load in loads:
        load.start()
    for load in loads[:4]:
        load.wait()

    margins = [geometry[0, my_row * 2 + r] for r in range(2)]
    offsets = [geometry[1, my_row * 2 + r] for r in range(2)]
    move = [jnp.where(upper, cols - offsets[r], 2 * cols - WIDE - margins[r] - offsets[r]) for r in range(2)]
    whole = [move[r] // LANES for r in range(2)]
    rest = [move[r] - whole[r] * LANES for r in range(2)]
    ri = lax.broadcasted_iota(jnp.int32, (vrows, vrows), 0)
    ci = lax.broadcasted_iota(jnp.int32, (vrows, vrows), 1)
    second = ri >= blocks
    a_id = jnp.where(second, ri - blocks, ri)
    a_id = a_id - jnp.where(second, whole[1], whole[0])
    a_id = jnp.where(a_id < 0, a_id + blocks, a_id)
    a_id = jnp.where(upper, blocks - 1 - a_id, a_id)
    pick = (ci == 2 * a_id + jnp.where(second, 1, 0)).astype(jnp.float32).astype(jnp.bfloat16)

    rl = lax.broadcasted_iota(jnp.int32, (vrows, LANES), 0)
    lane = lax.broadcasted_iota(jnp.int32, (vrows, LANES), 1)
    sec = rl >= blocks
    t = jnp.where(sec, rl - blocks, rl) * LANES + lane + jnp.where(upper, 0, WIDE - cols)
    offs = jnp.where(sec, offsets[1], offsets[0])
    marg = jnp.where(sec, margins[1], margins[0])
    ramp = ((t + offs - cols + marg).astype(jnp.float32) + 0.5) / marg.astype(jnp.float32)
    w = jnp.minimum(jnp.maximum(ramp, 0.0), 1.0)
    weight = jnp.where(upper, 1.0 - w, w)
    lane_b = lax.broadcasted_iota(jnp.int32, (blocks, LANES), 1)

    half_total = views * half
    base = s * views
    r128 = lax.broadcasted_iota(jnp.int32, (LANES, LANES), 0)
    c128 = lax.broadcasted_iota(jnp.int32, (LANES, LANES), 1)
    one = phase_ref[up]
    phases = []
    for r in range(2):
        to = r128 + rest[r]
        to = jnp.where(to >= LANES, to - LANES, to)
        turn = (to == c128).astype(jnp.float32).astype(jnp.bfloat16)
        turned = [dot(one[:, p * LANES:(p + 1) * LANES], turn) for p in range(3)]
        turned = jnp.concatenate(turned, axis=1).astype(jnp.bfloat16)
        phases.append(jnp.concatenate([turned] * 3, axis=0))

    def place(start):
        for v in range(paired):
            i = start + v
            src = jnp.where(upper, partner[base + i] - half_total - base, i)
            x = x_ref[jnp.minimum(jnp.maximum(src, 0), views - 1)]
            hi = x.astype(jnp.bfloat16)
            left = x - hi.astype(jnp.float32)
            md = left.astype(jnp.bfloat16)
            lo = (left - md.astype(jnp.float32)).astype(jnp.bfloat16)
            moved = dot(pick, jnp.concatenate([hi, md, lo], axis=1)).astype(jnp.bfloat16)
            for r in range(2):
                mv[r, v * blocks:(v + 1) * blocks, :] = moved[r * blocks:(r + 1) * blocks]
        for r in range(2):
            z[r] = dot(mv[r], phases[r])
        for v in range(paired):
            lines = []
            for r in range(2):
                rows = slice(v * blocks, (v + 1) * blocks)
                y = (
                    z[r, rows, :LANES]
                    + pltpu.roll(z[r, rows, LANES:2 * LANES], 1, 0)
                    + pltpu.roll(z[r, rows, 2 * LANES:], blocks - 1, 0)
                )
                y = -jnp.log(y * (1.0 / 3.0))
                y = jnp.where(lane_b < rest[r], pltpu.roll(y, 1, 0), y)
                lines.append(y)
            st[side, start + v] = weight * jnp.concatenate(lines, axis=0)

    def ex_copy(v):
        i = (1 - up) * paired + v
        return pltpu.make_async_remote_copy(
            src_ref=st.at[side, i], dst_ref=st.at[side, i],
            send_sem=ex_send.at[v], recv_sem=ex_recv.at[v],
            device_id={"views": other}, device_id_type=MESH)

    place(0)
    place(paired)

    for load in loads[4:]:
        load.wait()
    for k in range(NCOEF):
        acc = None
        for i in range(views):
            term = band[(base + i) * 16 + k] * st[side, i]
            acc = term if acc is None else acc + term
        cbuf[pl.ds(k, vrows, stride=SLOT), :] = acc
    cbuf[pl.ds(NCOEF, vrows, stride=SLOT), :] = jnp.zeros((vrows, LANES), jnp.float32)

    pl.semaphore_wait(barrier, n + nr - 2)

    def rs_copy(d):
        to = lax.rem(s + d + 1, half)
        return pltpu.make_async_remote_copy(
            src_ref=cbuf.at[pl.ds(pl.multiple_of(to * strip, 8), strip)], dst_ref=rsbuf.at[d],
            send_sem=rs_send.at[d], recv_sem=rs_recv.at[d],
            device_id={"views": up * half + to}, device_id_type=MESH)

    lap = 2 * blocks - TURNS
    per = strip // SLOT
    piece = min(per, lap)
    pieces = [(r * blocks + q * piece, r * blocks + blocks - lap + q * piece)
              for r in range(2) for q in range(lap // piece)]

    def lap_copy(m, e):
        low, high = pieces[m]
        return pltpu.make_async_remote_copy(
            src_ref=cbuf.at[pl.ds(low * SLOT, piece * SLOT)], dst_ref=lapbuf.at[e],
            send_sem=lap_send.at[m], recv_sem=lap_recv.at[e],
            device_id={"views": half + high // per}, device_id_type=MESH)

    each(half - 1, lambda d: rs_copy(d).start())

    @pl.when(jnp.logical_not(upper))
    def _():
        for m in range(len(pieces)):
            lap_copy(m, me).start()

    for v in range(paired // 2):
        ex_copy(v).start()
    agbuf[me] = cbuf[pl.ds(pl.multiple_of(s * strip, 8), strip), :]

    def rs_add(d):
        rs_copy(d).wait_recv()
        agbuf[me] = agbuf[me] + rsbuf[d]

    each(half - 1, rs_add)
    for m, (low, high) in enumerate(pieces):
        @pl.when(jnp.logical_and(upper, s == high // per))
        def _():
            at = pl.ds(high % per * SLOT, piece * SLOT)

            def lap_add(e):
                lap_copy(m, e).wait_recv()
                agbuf[me, at, :] = agbuf[me, at, :] + lapbuf[e]

            each(half, lap_add)

        @pl.when(jnp.logical_and(jnp.logical_not(upper), s == low // per))
        def _():
            agbuf[me, pl.ds(low % per * SLOT, piece * SLOT), :] = jnp.zeros((piece * SLOT, LANES), jnp.float32)

    par = lax.rem(me, 2)
    sibling = me + 1 - 2 * par

    def ag_copy(d, slot):
        return pltpu.make_async_remote_copy(
            src_ref=agbuf.at[slot], dst_ref=agbuf.at[slot],
            send_sem=ag_send.at[d], recv_sem=ag_recv.at[d],
            device_id={"views": lax.rem(me + 2 * d + 2, n)}, device_id_type=MESH)

    def fw_copy(d, slot):
        return pltpu.make_async_remote_copy(
            src_ref=agbuf.at[slot], dst_ref=agbuf.at[slot],
            send_sem=fw_send.at[d], recv_sem=fw_recv.at[d],
            device_id={"views": sibling}, device_id_type=MESH)

    def came(d):
        return lax.rem(me + n - 2 * d - 2, n)

    def came_sibling(d):
        return lax.rem(sibling + n - 2 * d - 2, n)

    def pw_copy(d):
        return pltpu.make_async_remote_copy(
            src_ref=pwbuf.at[0], dst_ref=pwbuf.at[d + 1],
            send_sem=pw_send.at[d], recv_sem=pw_recv.at[d],
            device_id={"rows": lax.rem(my_row + d + 1, nr)}, device_id_type=MESH)

    def pv_copy(d):
        return pltpu.make_async_remote_copy(
            src_ref=pvbuf.at[0], dst_ref=pvbuf.at[d + 1],
            send_sem=pv_send.at[d], recv_sem=pv_recv.at[d],
            device_id={"views": lax.rem(me + d + 1, n)}, device_id_type=MESH)

    each(half - 1, lambda d: ag_copy(d, me).start())
    fw_copy(half - 1, me).start()
    mine = agbuf[me]
    mine = mine * mine
    acc = mine[:SLOT]
    for q in range(1, per):
        acc = acc + mine[q * SLOT:(q + 1) * SLOT]
    pwbuf[0] = acc
    each(nr - 1, lambda d: pw_copy(d).start())
    for v in range(paired // 2, paired):
        ex_copy(v).start()
    each(half - 1, lambda d: rs_copy(d).wait_send())

    @pl.when(jnp.logical_not(upper))
    def _():
        for m in range(len(pieces)):
            lap_copy(m, me).wait_send()

    def forward(d):
        ag_copy(d, came(d)).wait_recv()
        fw_copy(d, came(d)).start()

    each(half - 1, forward)
    each(nr - 1, lambda d: pw_copy(d).wait_recv())
    acc = pwbuf[0]
    for d in range(nr - 1):
        acc = acc + pwbuf[d + 1]
    pvbuf[0] = acc
    each(n - 1, lambda d: pv_copy(d).start())
    fw_copy(half - 1, sibling).wait_recv()
    each(half - 1, lambda d: fw_copy(d, came_sibling(d)).wait_recv())
    each(half - 1, lambda d: ag_copy(d, me).wait_send())
    each(half - 1, lambda d: fw_copy(d, came(d)).wait_send())
    fw_copy(half - 1, me).wait_send()

    for k in range(NCOEF):
        sides = []
        for first_slot in (half, 0):
            got = [agbuf[first_slot + q, pl.ds(k, per, stride=SLOT), :] for q in range(half)]
            sides.append(jnp.concatenate(got, axis=0))
        for r in range(2):
            full[k, r] = jnp.concatenate([side_k[r * blocks:(r + 1) * blocks] for side_k in sides], axis=0)
    for v in range(paired):
        ex_copy(v).wait_send()
    for v in range(paired):
        i = up * paired + v
        pltpu.make_async_remote_copy(
            src_ref=st.at[1 - side, i], dst_ref=st.at[1 - side, i],
            send_sem=ex_send.at[v], recv_sem=ex_recv.at[v],
            device_id={"views": other}, device_id_type=MESH).wait_recv()
    each(n - 1, lambda d: pv_copy(d).wait_recv())
    total = pvbuf[0]
    if n <= 16:
        for d in range(n - 1):
            total = total + pvbuf[d + 1]
    else:
        total = lax.fori_loop(1, n, lambda d, c: c + pvbuf[d], total)
    total = jnp.sum(total, axis=1, keepdims=True)
    power = [total[g:g + 1] + (total[GBAND + g - 1:GBAND + g] if g else 0.0) for g in range(GBAND)]
    power = [p / (rows_total * WIDE) + SHRINK_FLOOR for p in power]
    for r in range(2):
        for g in range(GBAND):
            re = full[g, r]
            mag = re * re
            if g:
                im = full[GBAND + g - 1, r]
                mag = mag + im * im
            factor = (1.0 - (g / GBAND) ** 2) * mag / (mag + power[g])
            full[g, r] = factor * re
            if g:
                full[GBAND + g - 1, r] = factor * im
    each(nr - 1, lambda d: pw_copy(d).wait_send())
    each(n - 1, lambda d: pv_copy(d).wait_send())

    cos, sin = twist_ref[0], twist_ref[1]
    first = first_ref[...]
    for v in range(paired):
        i = up * paired + v
        lines = []
        for r in range(2):
            line = jnp.concatenate([st[0, i, r * blocks:(r + 1) * blocks],
                                    st[1, i, r * blocks:(r + 1) * blocks]], axis=0)
            for k in range(NCOEF):
                line = line - band[(base + i) * 16 + 8 + k] * full[k, r]
            lines.append(line)
        hi, lo = split(jnp.concatenate(lines, axis=1))
        step = dot(first, jnp.concatenate([hi, lo, hi], axis=0))
        for r in range(2):
            re = step[:PAD, r * LANES:(r + 1) * LANES]
            im = step[PAD:, r * LANES:(r + 1) * LANES]
            at = (2 * v + r) * PAD
            mid[at:at + PAD, :LANES] = re * cos + im * sin
            mid[at:at + PAD, LANES:] = im * cos - re * sin

    hi, lo = split(mid[...])
    spec = dot(hi, fwd_ref[0]) + dot(lo, fwd_ref[0]) + dot(hi, fwd_ref[1])
    resp = resp_ref[...]
    resp = jnp.concatenate([resp, resp], axis=1)
    resp = jnp.concatenate([resp] * (2 * paired), axis=0)
    hi, lo = split(spec * resp)
    mid[...] = dot(hi, inv_ref[0]) + dot(lo, inv_ref[0]) + dot(hi, inv_ref[1])

    last = last_ref[...]
    for v in range(paired):
        res, ims = [], []
        for r in range(2):
            at = (2 * v + r) * PAD
            re = mid[at:at + PAD, :LANES]
            im = mid[at:at + PAD, LANES:]
            res.append(re * cos - im * sin)
            ims.append(im * cos + re * sin)
        both = jnp.concatenate([jnp.concatenate(res, axis=1), jnp.concatenate(ims, axis=1)], axis=0)
        hi, lo = split(both)
        y = dot(last, jnp.concatenate([hi, lo, hi], axis=0))
        for r in range(2):
            out_ref[pl.ds(v * 2 * TURNS + r, TURNS, stride=2), :] = y[:TURNS, r * LANES:(r + 1) * LANES]


def on_device(n, nr, projections, partner, geometry):
    views, row_dev, cols = projections.shape
    assert row_dev == 2
    blocks = cols // LANES
    half = n // 2
    vrows = 2 * blocks
    strip = vrows * SLOT // half
    lap = 2 * blocks - TURNS
    piece = min(strip // SLOT, lap)
    x = projections.reshape(views, row_dev, blocks, LANES).transpose(0, 2, 1, 3).reshape(views, vrows, LANES)
    tables = (phase_table(),) + ramp_tables(blocks, TURNS - blocks)
    band = jnp.asarray(band_tables(views * half))
    vmem = pl.BlockSpec(memory_space=pltpu.VMEM)
    paired = views // 2
    dma = pltpu.SemaphoreType.DMA
    out = pl.pallas_call(
        functools.partial(kernel, n, nr, views, blocks, row_dev * nr),
        out_shape=jax.ShapeDtypeStruct((paired * 2 * TURNS, LANES), jnp.float32),
        in_specs=[pl.BlockSpec(memory_space=pl.ANY)] * (4 + len(tables)),
        out_specs=vmem,
        scratch_shapes=[
            pltpu.SMEM(partner.shape, jnp.int32),
            pltpu.SMEM(geometry.shape, jnp.int32),
            pltpu.SMEM(band.shape, jnp.float32),
            pltpu.VMEM(x.shape, jnp.float32),
            *[pltpu.VMEM(t.shape, t.dtype) for t in tables],
            dma((4 + len(tables),)),
            pltpu.VMEM((2, views, vrows, LANES), jnp.float32),
            pltpu.VMEM((vrows * SLOT, LANES), jnp.float32),
            pltpu.VMEM((half - 1, strip, LANES), jnp.float32),
            pltpu.VMEM((n, strip, LANES), jnp.float32),
            pltpu.VMEM((NCOEF, 2, 2 * blocks, LANES), jnp.float32),
            pltpu.VMEM((nr, SLOT, LANES), jnp.float32),
            pltpu.VMEM((n, SLOT, LANES), jnp.float32),
            pltpu.VMEM((half, piece * SLOT, LANES), jnp.float32),
            pltpu.VMEM((paired * 2 * PAD, 2 * LANES), jnp.float32),
            pltpu.VMEM((2, paired * blocks, 3 * LANES), jnp.bfloat16),
            pltpu.VMEM((2, paired * blocks, 3 * LANES), jnp.float32),
            dma((paired,)), dma((paired,)),
            dma((half - 1,)), dma((half - 1,)),
            dma((half - 1,)), dma((half - 1,)),
            dma((half,)), dma((half,)),
            dma((nr - 1,)), dma((nr - 1,)),
            dma((n - 1,)), dma((n - 1,)),
            dma((2 * (lap // piece),)), dma((half,)),
        ],
        compiler_params=pltpu.CompilerParams(
            collective_id=0, has_side_effects=True, vmem_limit_bytes=56 * 2**20),
        cost_estimate=pl.CostEstimate(flops=10**9, bytes_accessed=2 * 10**6, transcendentals=131072),
    )(partner, geometry, band, x, *[jnp.asarray(t) for t in tables])
    out = out.reshape(paired, TURNS, 2, LANES).transpose(0, 2, 1, 3)
    out = with_layout_constraint(out, Layout(major_to_minor=(0, 2, 1, 3)))
    return out.reshape(paired, 2, WIDE)


def solution(mesh):
    in_specs = (P("views", "rows", None), P(), P())
    out_specs = P("views", "rows", None)
    n, nr = mesh.shape["views"], mesh.shape["rows"]
    return jax.shard_map(
        functools.partial(on_device, n, nr), mesh=mesh, in_specs=in_specs, out_specs=out_specs, check_vma=False
    )
```
